256 devices in a mesh: wide: 32 (over x_hi, z, core), narrow: 8 (over x_lo, y).
Axes of the slice: x: 4 (x_hi: 2, x_lo: 2; x = x_hi * 2 + x_lo), y: 4, z: 8, core: 2. Of those that a mesh axis runs over, the one named last changes fastest.
Arguments:
- field: bfloat16 [20, 256, 256, 256], P(None, 'wide', 'narrow'), may hold values from -6 to 6
- cotangent: bfloat16 [20, 256, 256, 256], P(None, 'wide', 'narrow'), may hold values from -6 to 6
- spectral_weight: float32 [2, 20, 20, 32, 32, 32], P(None, None, None, 'narrow', None, 'wide'), may hold values from -18 to 18
- local_weight: bfloat16 [20, 20], replicated, may hold values from -1.25 to 1.25
- local_bias: float32 [20], replicated, may hold values from -3 to 3
Outputs:
- activated: bfloat16 [20, 256, 256, 256], P(None, 'wide', 'narrow')
- field_grad: bfloat16 [20, 256, 256, 256], P(None, 'wide', 'narrow')
- weight_grad: float32 [2, 20, 20, 32, 32, 32], P(None, None, None, 'narrow', None, 'wide')
The draws below stay inside these ranges and needn't reach their ends.
All inputs are finite; a program needn't handle non-finite values.
Results may differ from the reference program's by a relative error of at most 0.022.
Values may be sent and summed in bfloat16 or wider, within the bound.
No kernel may reach another device: no remote copies, remote signals or barrier semaphores. Data moves between devices by JAX's collectives and lax.ppermute only.
A program may use at most 128 MiB of HBM per device.

```python
import math
import jax
import jax.numpy as jnp
from jax import lax

N = 256
C = 20
M = 32


def block_levels(rng, dims, pieces, least, top_value):
    gain = 1.0
    for dim, shards_of in pieces:
        steps = jax.random.uniform(jax.random.fold_in(jax.random.fold_in(rng, 6), dim), (shards_of,), jnp.float32, least / len(pieces), top_value / len(pieces))
        gain = gain * jnp.repeat(jnp.exp(steps), dims[dim] // shards_of).reshape((-1,) + (1,) * (len(dims) - 1 - dim))
    return gain


def centred(stream_key, shape, deviation, limit, pieces=(), kind=jnp.bfloat16):
    values = deviation * jax.random.normal(stream_key, shape, jnp.float32)
    if pieces:
        values = values * block_levels(stream_key, shape, pieces, -0.22, 0.18)
    return jnp.clip(values, -limit, limit).astype(kind)


def setup_inputs(seed: int = 0) -> dict:
    key_of = jax.random.split(jax.random.key(seed), 6)
    field = centred(key_of[0], (C, N, N, N), 1.0, 6.0, ((1, 32), (2, 8)))
    cotangent = centred(key_of[1], (C, N, N, N), 1.0, 6.0, ((1, 32), (2, 8)))
    spectral_weight = centred(key_of[2], (2, C, C, M, M, M), 3.0, 18.0, ((3, 8), (5, 32)), jnp.float32)
    local_weight = centred(key_of[3], (C, C), C ** -0.5, 1.25)
    local_bias = centred(key_of[4], (C,), 0.5, 3.0, (), jnp.float32)
    return {"field": field, "cotangent": cotangent, "spectral_weight": spectral_weight, "local_weight": local_weight, "local_bias": local_bias}


def tables():
    index = jnp.arange(N, dtype=jnp.int32)
    depth_freq = jnp.arange(M, dtype=jnp.int32)
    lateral_freq = jnp.where(depth_freq < M // 2, depth_freq, N - M + depth_freq).astype(jnp.int32)
    scale = 1.0 / math.sqrt(N)

    def angles(freqs):
        return 2.0 * math.pi / N * (freqs[:, None] * index[None, :] % N).astype(jnp.float32)
    depth_angle = angles(depth_freq)
    weights = jnp.where(depth_freq == 0, 1.0, 2.0).astype(jnp.float32)[:, None]
    depth_forward = (jnp.concatenate([jnp.cos(depth_angle), -jnp.sin(depth_angle)], axis=0) * scale).T.astype(jnp.bfloat16)
    depth_inverse = (jnp.concatenate([weights * jnp.cos(depth_angle), -weights * jnp.sin(depth_angle)], axis=0) * scale).astype(jnp.bfloat16)
    lateral_angle = angles(lateral_freq)
    cosine = jnp.cos(lateral_angle) * scale
    sine = jnp.sin(lateral_angle) * scale

    def complex_form(real_part, imag_part):
        return jnp.stack([jnp.stack([real_part, imag_part]), jnp.stack([-imag_part, real_part])])
    lateral_forward = jnp.transpose(complex_form(cosine, -sine), (0, 3, 1, 2)).astype(jnp.bfloat16)
    lateral_inverse = jnp.transpose(complex_form(cosine, sine), (0, 2, 1, 3)).astype(jnp.bfloat16)
    return (depth_forward, depth_inverse, lateral_forward, lateral_inverse)

def mix(spectrum, weight):

    def product(left, right):
        return jnp.einsum('cijk,coijk->oijk', left, right, precision=lax.Precision.HIGHEST)
    real_part = product(spectrum[0], weight[0]) - product(spectrum[1], weight[1])
    imag_part = product(spectrum[0], weight[1]) + product(spectrum[1], weight[0])
    return jnp.stack([real_part, imag_part])

def mix_back(response, weight):

    def product(left, right):
        return jnp.einsum('oijk,coijk->cijk', left, right, precision=lax.Precision.HIGHEST)
    real_part = product(response[0], weight[0]) + product(response[1], weight[1])
    imag_part = product(response[1], weight[0]) - product(response[0], weight[1])
    return jnp.stack([real_part, imag_part])

def outer(spectrum, response):

    def product(left, right):
        return left[:, None] * right[None, :]
    real_part = product(spectrum[0], response[0]) + product(spectrum[1], response[1])
    imag_part = product(spectrum[0], response[1]) - product(spectrum[1], response[0])
    return jnp.stack([real_part, imag_part])

def analyse(values, depth_table, lateral):
    flat = jnp.dot(values.reshape(-1, N), depth_table, preferred_element_type=jnp.float32)
    planes = flat.astype(jnp.bfloat16).reshape(C, N, N, 2, M).astype(jnp.float32)
    table = lateral.astype(jnp.float32)
    partial_sum = jnp.einsum('cxyrk,rxsi->cysik', planes, table, precision=lax.Precision.HIGHEST)
    return jnp.einsum('cyrik,rysj->scijk', partial_sum, table, precision=lax.Precision.HIGHEST)

def synthesise(spectrum, lateral):
    table = lateral.astype(jnp.float32)
    values = spectrum.astype(jnp.float32)
    lines = jnp.einsum('rcijk,rjsy->cysik', values, table, precision=lax.Precision.HIGHEST)
    return jnp.einsum('cyrik,risx->cxysk', lines, table, precision=lax.Precision.HIGHEST).astype(jnp.bfloat16)

def reference(field, cotangent, spectral_weight, local_weight, local_bias):
    depth_forward, depth_inverse, lateral_forward, lateral_inverse = tables()
    spectrum = analyse(field, depth_forward, lateral_forward)
    mixed = mix(spectrum, spectral_weight).astype(jnp.bfloat16)
    planes = synthesise(mixed, lateral_inverse)
    field_rows = field.reshape(C, -1)

    def forward_channel(index):
        spatial = jnp.dot(planes[index].reshape(-1, 2 * M), depth_inverse, preferred_element_type=jnp.float32).reshape(N, N, N)
        local_term = jnp.dot(local_weight[index], field_rows, preferred_element_type=jnp.float32).reshape(N, N, N)
        before_gelu = spatial + local_term + local_bias[index]
        activated, pullback = jax.vjp(jax.nn.gelu, before_gelu)
        slope = pullback(cotangent[index].astype(jnp.float32))[0]
        return (activated.astype(jnp.bfloat16), slope.astype(jnp.bfloat16))
    activated, slope = lax.map(forward_channel, jnp.arange(C, dtype=jnp.int32))
    response = analyse(slope, depth_inverse.T, lateral_forward)
    weight_grad = outer(spectrum, response)
    returned = mix_back(response, spectral_weight).astype(jnp.bfloat16)
    back_planes = synthesise(returned, lateral_inverse)
    slope_rows = slope.reshape(C, -1)

    def grad_channel(index):
        spatial = jnp.dot(back_planes[index].reshape(-1, 2 * M), depth_forward.T, preferred_element_type=jnp.float32).reshape(N, N, N)
        local_term = jnp.dot(local_weight[:, index], slope_rows, preferred_element_type=jnp.float32).reshape(N, N, N)
        return (spatial + local_term).astype(jnp.bfloat16)
    field_grad = lax.map(grad_channel, jnp.arange(C, dtype=jnp.int32))
    return (activated, field_grad, weight_grad)
```

```python
import math

import jax
import jax.numpy as jnp
import ml_dtypes
import numpy as np
from jax import lax
from jax.experimental import pallas as pl
from jax.experimental.pallas import tpu as pltpu
from jax.sharding import PartitionSpec as P

N = 256
M = 32
C = 20
CP = 24
BF = jnp.bfloat16
F32 = jnp.float32
MIB = 1024 * 1024


def depth_tables():
    index = np.arange(N)
    freq = np.arange(M)
    angle = (2.0 * math.pi / N) * ((freq[:, None] * index[None, :]) % N)
    scale = 1.0 / math.sqrt(N)
    weights = np.where(freq == 0, 1.0, 2.0)[:, None]
    forward = (np.concatenate([np.cos(angle), -np.sin(angle)]) * scale).T
    inverse = np.concatenate([weights * np.cos(angle), -weights * np.sin(angle)]) * scale
    return forward, inverse


def lateral_angles():
    index = np.arange(N)
    base = np.arange(M)
    freq = np.where(base < M // 2, base, N - M + base)
    angle = (2.0 * math.pi / N) * ((freq[:, None] * index[None, :]) % N)
    scale = 1.0 / math.sqrt(N)
    return np.cos(angle) * scale, np.sin(angle) * scale


def bf16(array):
    return np.asarray(array, np.float32).astype(ml_dtypes.bfloat16)


def analysis_depth(table):
    out = np.zeros((2, N, 2, 2, 2, M))
    for half in range(2):
        real, imag = table[:, :M], table[:, M:]
        out[half, :, 0, 0, half] = real
        out[half, :, 0, 1, half] = imag
        out[half, :, 1, 0, half] = imag
        out[half, :, 1, 1, half] = -real
    return bf16(out.reshape(2, N, 256))


def synthesis_depth(table):
    out = np.zeros((2, 2, M, 2, N))
    for half in range(2):
        out[:, half, :, half] = table.reshape(2, M, N)
    return bf16(out.reshape(128, 512))


def second_tables():
    cosine, sine = lateral_angles()
    out = np.zeros((8, 8, 4, 4, 2, 4, M))
    for block in range(8):
        rows = slice(block * M, (block + 1) * M)
        for x in range(4):
            out[block, :, :, x, 0, x] = cosine[:, rows].reshape(8, 4, M)
            out[block, :, :, x, 1, x] = sine[:, rows].reshape(8, 4, M)
    out = out.reshape(8, 128, 256)
    return bf16(out), bf16(out.transpose(0, 2, 1))


def first_tables():
    cosine, sine = lateral_angles()
    cos_x = cosine.T.reshape(M, 8, M)
    sin_x = sine.T.reshape(M, 8, M)
    forward = np.zeros((M, 2, 8, 2, 4, M))
    inverse = np.zeros((M, 2, 8, 2, 4, M))
    for j in range(4):
        forward[:, 0, :, 0, j] = cos_x
        forward[:, 0, :, 1, j] = -sin_x
        forward[:, 1, :, 0, j] = sin_x
        forward[:, 1, :, 1, j] = cos_x
        inverse[:, 0, :, 0, j] = cos_x
        inverse[:, 0, :, 1, j] = -sin_x
        inverse[:, 1, :, 0, j] = sin_x
        inverse[:, 1, :, 1, j] = cos_x
    return bf16(forward.reshape(512, 256)), bf16(inverse.reshape(512, 256))


def permutation(rows, lanes, sizes):
    total = int(np.prod([sizes[d] for d in rows]))
    position = np.arange(total).reshape([sizes[d] for d in rows])
    order = position.transpose([rows.index(d) for d in lanes]).reshape(-1)
    out = np.zeros((total, total))
    out[order, np.arange(total)] = 1.0
    return bf16(out)


def dot(a, b):
    return jnp.dot(a, b, preferred_element_type=F32)


def dot_nt(a, b):
    return lax.dot_general(a, b, (((1,), (1,)), ((), ())), preferred_element_type=F32)


def dot_tn(a, b):
    return lax.dot_general(a, b, (((0,), (0,)), ((), ())), preferred_element_type=F32)


def params(limit=40):
    return pltpu.CompilerParams(vmem_limit_bytes=limit * MIB)


def cost(flops, bytes_accessed, transcendentals=0):
    return pl.CostEstimate(
        flops=flops, bytes_accessed=bytes_accessed, transcendentals=transcendentals
    )


def second_forward(planes_ref, table, out_ref, first, count):
    for c in range(0, count, 2):
        one = planes_ref[first + c]
        two = planes_ref[first + c + 1]
        stacked = jnp.concatenate(
            [
                jnp.concatenate([one[:, :128], two[:, :128]], axis=1),
                jnp.concatenate([one[:, 128:], two[:, 128:]], axis=1),
            ],
            axis=0,
        )
        got = dot(table, stacked).astype(BF)
        for q in range(2):
            out_ref[:, (c + q) * 16 : (c + q + 1) * 16, :] = got[
                :, q * 128 : (q + 1) * 128
            ].reshape(8, 16, 128)


def analyse_kernel(field_ref, depth_ref, table_ref, out_ref, planes_ref):
    count = field_ref.shape[0]
    low = field_ref[:, 0].reshape(count * 128, N)
    high = field_ref[:, 1].reshape(count * 128, N)
    planes = dot(low, depth_ref[0]) + dot(high, depth_ref[1])
    planes_ref[...] = planes.astype(BF).reshape(count, 128, N)
    second_forward(planes_ref, table_ref[...], out_ref, 0, count)


def analyse(field, depth, table):
    step = 4
    return pl.pallas_call(
        analyse_kernel,
        grid=(C // step,),
        in_specs=[
            pl.BlockSpec((step, 2, 4, M, N), lambda t: (t, 0, 0, 0, 0)),
            pl.BlockSpec((2, N, 256), lambda t: (0, 0, 0)),
            pl.BlockSpec((128, 256), lambda t: (0, 0)),
        ],
        out_specs=pl.BlockSpec((8, step * 16, 128), lambda t: (0, t, 0)),
        out_shape=jax.ShapeDtypeStruct((8, C * 16, 128), BF),
        scratch_shapes=[pltpu.VMEM((step, 128, 256), BF)],
        compiler_params=params(),
        cost_estimate=cost(2 * 20 * 256 * 256 * 256, 3 * MIB),
        name="analyse",
    )(field, depth, table)


def gather_kernel(in_ref, perm_ref, out_ref, sum_ref, rows_ref, turned_ref):
    total = in_ref[0].astype(F32)
    for source in range(1, 8):
        total = total + in_ref[source].astype(F32)
    sum_ref[0 : C * 16] = total
    sum_ref[C * 16 :] = jnp.zeros((64, 128), F32)
    rows_ref[...] = jnp.zeros((512, 128), F32)
    for x in range(4):
        for j in range(4):
            rows_ref[x * 128 + j * 32 : x * 128 + j * 32 + CP, :] = sum_ref[
                pl.ds(j * 4 + x, CP, stride=16), :
            ]
    got = dot_nt(perm_ref[...], rows_ref[...].astype(BF))
    for x in range(4):
        turned_ref[pl.ds(x, 128, stride=4), :] = got[:, x * 128 : (x + 1) * 128]
    out_ref[...] = turned_ref[...].astype(BF).reshape(32, 16, 128)


def gather(parts, perm):
    return pl.pallas_call(
        gather_kernel,
        out_shape=jax.ShapeDtypeStruct((32, 16, 128), BF),
        scratch_shapes=[
            pltpu.VMEM((C * 16 + 64, 128), F32),
            pltpu.VMEM((512, 128), F32),
            pltpu.VMEM((512, 128), F32),
        ],
        compiler_params=params(),
        cost_estimate=cost(2 * 128 * 128 * 512, MIB),
        name="gather",
    )(parts, perm)


def scatter_kernel(in_ref, perm_ref, out_ref, turned_ref, rows_ref):
    turned_ref[...] = in_ref[...].reshape(512, 128).astype(F32)
    for x in range(4):
        block = turned_ref[pl.ds(x, 128, stride=4), :].astype(BF)
        got = dot_tn(block, perm_ref[...])
        for j in range(4):
            rows_ref[pl.ds(j * 4 + x, CP, stride=16), :] = got[j * 32 : j * 32 + CP]
    value = rows_ref[0 : C * 16].astype(BF)
    for target in range(8):
        out_ref[target] = value


def scatter(lines, perm):
    return pl.pallas_call(
        scatter_kernel,
        out_shape=jax.ShapeDtypeStruct((8, C * 16, 128), BF),
        scratch_shapes=[
            pltpu.VMEM((512, 128), F32),
            pltpu.VMEM((CP * 16, 128), F32),
        ],
        compiler_params=params(),
        cost_estimate=cost(2 * 128 * 128 * 512, MIB),
        name="scatter",
    )(lines, perm)


def lane_group(shape):
    return lax.broadcasted_iota(jnp.int32, shape, 1) // M % 4


def to_modes(lines_ref, first_ref):
    got = dot_tn(lines_ref[...].reshape(512, 128), first_ref[...])
    group = lane_group((M, 256))
    out = jnp.zeros((M, 256), F32)
    for j in range(4):
        out = jnp.where(group == j, got[j * M : (j + 1) * M], out)
    return out[:, :128], out[:, 128:]


def from_modes(real, imag, inverse_ref, out_ref):
    both = jnp.concatenate([real, imag], axis=1)
    group = lane_group((M, 256))
    rows = [jnp.where(group == j, both, 0.0) for j in range(4)]
    stacked = jnp.concatenate(rows, axis=0).astype(BF)
    out_ref[...] = dot_nt(inverse_ref[...], stacked).astype(BF).reshape(32, 16, 128)


def mix_kernel(lines_ref, weight_ref, first_ref, inverse_ref, out_ref, spectrum_ref):
    real, imag = to_modes(lines_ref, first_ref)
    spectrum_ref[0] = real
    spectrum_ref[1] = imag
    mixed_real = jnp.zeros((CP, 128), F32)
    mixed_imag = jnp.zeros((CP, 128), F32)
    for c in range(C):
        w0 = weight_ref[c * CP : (c + 1) * CP, :]
        w1 = weight_ref[(C + c) * CP : (C + c + 1) * CP, :]
        s0 = real[c : c + 1]
        s1 = imag[c : c + 1]
        mixed_real = mixed_real + s0 * w0 - s1 * w1
        mixed_imag = mixed_imag + s0 * w1 + s1 * w0
    pad = jnp.zeros((M - CP, 128), F32)
    from_modes(
        jnp.concatenate([mixed_real, pad]),
        jnp.concatenate([mixed_imag, pad]),
        inverse_ref,
        out_ref,
    )


def mix_back_kernel(
    lines_ref, weight_ref, first_ref, inverse_ref, spectrum_ref, perm_ref, out_ref, pair_ref, acc_ref
):
    real, imag = to_modes(lines_ref, first_ref)
    both = jnp.concatenate([spectrum_ref[0], spectrum_ref[1], real, imag], axis=0)
    pair_ref[...] = dot_nt(perm_ref[...], both.astype(BF)).astype(BF).reshape(8, 16, 128)
    r0 = real[:CP]
    r1 = imag[:CP]
    acc_ref[...] = jnp.zeros((2, M, 128), F32)
    for c in range(C):
        w0 = weight_ref[c * CP : (c + 1) * CP, :]
        w1 = weight_ref[(C + c) * CP : (C + c + 1) * CP, :]
        acc_ref[0, c : c + 1, :] = jnp.sum(r0 * w0 + r1 * w1, axis=0, keepdims=True)
        acc_ref[1, c : c + 1, :] = jnp.sum(r1 * w0 - r0 * w1, axis=0, keepdims=True)
    from_modes(acc_ref[0], acc_ref[1], inverse_ref, out_ref)


def mix(lines, weight, first, inverse):
    return pl.pallas_call(
        mix_kernel,
        out_shape=[
            jax.ShapeDtypeStruct((32, 16, 128), BF),
            jax.ShapeDtypeStruct((2, M, 128), F32),
        ],
        compiler_params=params(),
        cost_estimate=cost(4 * 512 * 128 * 256, 2 * MIB),
        name="mix",
    )(lines, weight, first, inverse)


def mix_back(lines, weight, first, inverse, spectrum, perm):
    return pl.pallas_call(
        mix_back_kernel,
        out_shape=[
            jax.ShapeDtypeStruct((32, 16, 128), BF),
            jax.ShapeDtypeStruct((8, 16, 128), BF),
        ],
        scratch_shapes=[pltpu.VMEM((2, M, 128), F32)],
        compiler_params=params(),
        cost_estimate=cost(4 * 512 * 128 * 256, 2 * MIB),
        name="mix_back",
    )(lines, weight, first, inverse, spectrum, perm)


def weight_out_kernel(weight_ref, perm_ref, out_ref, rows_ref):
    for q in range(2 * C):
        rows_ref[q * CP : q * CP + C, :] = weight_ref[q]
        rows_ref[q * CP + C : (q + 1) * CP, :] = jnp.zeros((CP - C, 128), F32)
    got = dot_nt(perm_ref[...], rows_ref[...].astype(BF))
    out_ref[...] = got.astype(BF).reshape(8, 16, 2 * C * CP)


def weight_out(weight, perm):
    return pl.pallas_call(
        weight_out_kernel,
        out_shape=jax.ShapeDtypeStruct((8, 16, 2 * C * CP), BF),
        scratch_shapes=[pltpu.VMEM((2 * C * CP, 128), F32)],
        compiler_params=params(),
        cost_estimate=cost(2 * 128 * 128 * 960, MIB),
        name="weight_out",
    )(weight, perm)


def weight_in_kernel(in_ref, perm_ref, out_ref):
    out_ref[...] = dot_tn(in_ref[...].reshape(128, 2 * C * CP), perm_ref[...])


def weight_in(parts, perm):
    return pl.pallas_call(
        weight_in_kernel,
        out_shape=jax.ShapeDtypeStruct((2 * C * CP, 128), F32),
        compiler_params=params(),
        cost_estimate=cost(2 * 128 * 128 * 960, MIB),
        name="weight_in",
    )(parts, perm)


def outer_kernel(pair_ref, perm_ref, out_ref):
    modes = dot_tn(pair_ref[...].reshape(128, 128), perm_ref[...])
    s0, s1 = modes[0:M], modes[M : 2 * M]
    r0, r1 = modes[2 * M : 2 * M + C], modes[3 * M : 3 * M + C]
    for c in range(C):
        a, b = s0[c : c + 1], s1[c : c + 1]
        out_ref[0, c] = a * r0 + b * r1
        out_ref[1, c] = a * r1 - b * r0


def outer(pair, perm):
    return pl.pallas_call(
        outer_kernel,
        out_shape=jax.ShapeDtypeStruct((2, C, C, 128), F32),
        compiler_params=params(),
        cost_estimate=cost(2 * 128 * 128 * 128, MIB),
        name="outer",
    )(pair, perm)


def second_inverse(in_ref, table_ref, planes_ref):
    table = table_ref[...]
    lane = lax.broadcasted_iota(jnp.int32, (128, 256), 1) % 128
    for c in range(0, C, 2):
        both = jnp.concatenate(
            [in_ref[:, (c + q) * 16 : (c + q + 1) * 16, :].reshape(128, 128) for q in range(2)],
            axis=1,
        )
        got = dot(table, both)
        for q in range(2):
            cos_part = got[:128, q * 128 : (q + 1) * 128]
            sin_part = got[128:, q * 128 : (q + 1) * 128]
            turned = pltpu.roll(sin_part, 64, 1)
            value = jnp.where(lane[:, :128] < 64, cos_part - turned, cos_part + turned)
            planes_ref[c + q] = value.astype(BF)


def local_kernel(
    parts_ref,
    field_ref,
    cotangent_ref,
    inverse_ref,
    synth_ref,
    depth_ref,
    table_ref,
    local_ref,
    bias_ref,
    activated_ref,
    slope_ref,
    out_ref,
    planes_ref,
    turned_ref,
):
    step = pl.program_id(0)

    @pl.when(step == 0)
    def _():
        second_inverse(parts_ref, inverse_ref, planes_ref)

    rows = pl.ds(pl.multiple_of(step * 16, 16), 16)
    planes = planes_ref[:, rows, :].reshape(C * 16, 128)
    spatial = dot(planes, synth_ref[...])
    response = jnp.zeros((C * 16, 256), F32)
    for x in range(2):
        field = field_ref[:, x].reshape(C * 16, N)
        value = spatial[:, x * N : (x + 1) * N] + dot(local_ref[...], field) + bias_ref[...]
        square = value * value
        inner = value * (0.7978845608028654 + 0.7978845608028654 * 0.044715 * square)
        tanh = jnp.tanh(inner)
        half = 0.5 + 0.5 * tanh
        activated = value * half
        d_inner = 0.7978845608028654 + 3.0 * 0.7978845608028654 * 0.044715 * square
        d_gelu = half + (0.5 * value) * (1.0 - tanh * tanh) * d_inner
        cotangent = cotangent_ref[:, x].reshape(C * 16, N).astype(F32)
        slope = (cotangent * d_gelu).astype(BF)
        activated_ref[:, x] = activated.astype(BF).reshape(C, 16, N)
        slope_ref[:, x] = slope.reshape(C, 16, N)
        response = response + dot(slope, depth_ref[x])
    turned_ref[:, rows, :] = response.astype(BF).reshape(C, 16, 256)

    @pl.when(step == pl.num_programs(0) - 1)
    def _():
        second_forward(turned_ref, table_ref[...], out_ref, 0, C)


def whole(shape):
    return pl.BlockSpec(shape, lambda t: (0,) * len(shape))


GRID_BLOCK = (C, 2, None, 16, N)


def grid_spec():
    return pl.BlockSpec(GRID_BLOCK, lambda t: (0, 0, t // 2, t % 2, 0))


def local(parts, field, cotangent, inverse, synth, depth, table, weight, bias):
    grid_shape = jax.ShapeDtypeStruct((C, 2, 4, M, N), BF)
    return pl.pallas_call(
        local_kernel,
        grid=(8,),
        in_specs=[
            whole((8, C * 16, 128)),
            grid_spec(),
            grid_spec(),
            whole((256, 128)),
            whole((128, 512)),
            whole((2, N, 256)),
            whole((128, 256)),
            whole((C * 16, C * 16)),
            whole((C * 16, N)),
        ],
        out_specs=[grid_spec(), grid_spec(), whole((8, C * 16, 128))],
        out_shape=[grid_shape, grid_shape, jax.ShapeDtypeStruct((8, C * 16, 128), BF)],
        scratch_shapes=[pltpu.VMEM((C, 128, 128), BF), pltpu.VMEM((C, 128, 256), BF)],
        compiler_params=params(),
        cost_estimate=cost(3 * 10**9, 12 * MIB, 1310720),
        name="local",
    )(parts, field, cotangent, inverse, synth, depth, table, weight, bias)


def local_back_kernel(
    parts_ref, slope_ref, inverse_ref, synth_ref, local_ref, out_ref, planes_ref
):
    step = pl.program_id(0)

    @pl.when(step == 0)
    def _():
        second_inverse(parts_ref, inverse_ref, planes_ref)

    rows = pl.ds(pl.multiple_of(step * 16, 16), 16)
    planes = planes_ref[:, rows, :].reshape(C * 16, 128)
    spatial = dot(planes, synth_ref[...])
    for x in range(2):
        slope = slope_ref[:, x].reshape(C * 16, N)
        value = spatial[:, x * N : (x + 1) * N] + dot(local_ref[...], slope)
        out_ref[:, x] = value.astype(BF).reshape(C, 16, N)


def local_back(parts, slope, inverse, synth, weight):
    return pl.pallas_call(
        local_back_kernel,
        grid=(8,),
        in_specs=[
            whole((8, C * 16, 128)),
            grid_spec(),
            whole((256, 128)),
            whole((128, 512)),
            whole((C * 16, C * 16)),
        ],
        out_specs=grid_spec(),
        out_shape=jax.ShapeDtypeStruct((C, 2, 4, M, N), BF),
        scratch_shapes=[pltpu.VMEM((C, 128, 128), BF)],
        compiler_params=params(),
        cost_estimate=cost(2 * 10**9, 6 * MIB),
        name="local_back",
    )(parts, slope, inverse, synth, weight)


def exchange(value, axis):
    return lax.all_to_all(value, axis, split_axis=0, concat_axis=0, tiled=True)


def shards(field, cotangent, spectral_weight, local_weight, local_bias):
    forward, inverse = depth_tables()
    forward_b, inverse_b = analysis_depth(forward), analysis_depth(inverse.T)
    synth_f, synth_b = synthesis_depth(inverse), synthesis_depth(forward.T)
    second, second_back = second_tables()
    first, first_back = first_tables()
    block = lax.axis_index("narrow")
    table = lax.dynamic_index_in_dim(jnp.asarray(second), block, 0, keepdims=False)
    table_back = lax.dynamic_index_in_dim(jnp.asarray(second_back), block, 0, keepdims=False)

    sizes = {"s": 2, "p": 2, "k": 32, "J": 8, "j": 4, "i": 4}
    perm_line = permutation("ksp", "spk", sizes)
    perm_weight = permutation("Jji", "iJj", sizes)
    perm_modes = permutation("Jji", "jJi", sizes)
    spread = np.zeros((C * 16, C))
    spread[np.arange(C * 16), np.arange(C * 16) // 16] = 1.0
    same = np.equal(np.arange(C * 16)[:, None] % 16, np.arange(C * 16)[None, :] % 16)
    spread, same = jnp.asarray(bf16(spread)), jnp.asarray(bf16(same))
    wide_weight = jnp.dot(jnp.dot(spread, local_weight), spread.T) * same
    wide_weight_back = wide_weight.T
    bias = jnp.broadcast_to(jnp.repeat(local_bias, 16)[:, None], (C * 16, N))

    shape = field.shape
    grid_field = field.reshape(C, 2, 4, M, N)
    grid_cotangent = cotangent.reshape(C, 2, 4, M, N)

    weight = weight_in(
        exchange(weight_out(spectral_weight.reshape(2 * C, C, 128), perm_weight), "narrow"),
        perm_modes,
    )
    parts = exchange(analyse(grid_field, forward_b, table), "narrow")
    lines = exchange(gather(parts, perm_line), "wide")
    lines, spectrum = mix(lines, weight, first, first_back)
    lines = exchange(lines, "wide")
    parts = exchange(scatter(lines, perm_line), "narrow")
    activated, slope, parts = local(
        parts,
        grid_field,
        grid_cotangent,
        table_back,
        synth_f,
        inverse_b,
        table,
        wide_weight,
        bias,
    )
    parts = exchange(parts, "narrow")
    lines = exchange(gather(parts, perm_line), "wide")
    lines, pair = mix_back(lines, weight, first, first_back, spectrum, perm_modes)
    lines = exchange(lines, "wide")
    weight_grad = outer(exchange(pair, "narrow"), perm_weight)
    parts = exchange(scatter(lines, perm_line), "narrow")
    field_grad = local_back(parts, slope, table_back, synth_b, wide_weight_back)
    return (
        activated.reshape(shape),
        field_grad.reshape(shape),
        weight_grad.reshape(spectral_weight.shape),
    )


def solution(mesh):
    return jax.shard_map(
        shards,
        mesh=mesh,
        in_specs=(
            P(None, "wide", "narrow", None),
            P(None, "wide", "narrow", None),
            P(None, None, None, "narrow", None, "wide"),
            P(),
            P(),
        ),
        out_specs=(
            P(None, "wide", "narrow", None),
            P(None, "wide", "narrow", None),
            P(None, None, None, "narrow", None, "wide"),
        ),
        check_vma=False,
    )
```

```python
import functools
import math

import jax
import jax.numpy as jnp
import ml_dtypes
import numpy as np
from jax import lax
from jax.experimental import pallas as pl
from jax.experimental.pallas import tpu as pltpu
from jax.sharding import PartitionSpec as P

N = 256
M = 32
C = 20
CP = 24
BF = jnp.bfloat16
F32 = jnp.float32
MIB = 1024 * 1024


def depth_tables():
    index = np.arange(N)
    freq = np.arange(M)
    angle = (2.0 * math.pi / N) * ((freq[:, None] * index[None, :]) % N)
    scale = 1.0 / math.sqrt(N)
    weights = np.where(freq == 0, 1.0, 2.0)[:, None]
    forward = (np.concatenate([np.cos(angle), -np.sin(angle)]) * scale).T
    inverse = np.concatenate([weights * np.cos(angle), -weights * np.sin(angle)]) * scale
    return forward, inverse


def lateral_angles():
    index = np.arange(N)
    base = np.arange(M)
    freq = np.where(base < M // 2, base, N - M + base)
    angle = (2.0 * math.pi / N) * ((freq[:, None] * index[None, :]) % N)
    scale = 1.0 / math.sqrt(N)
    return np.cos(angle) * scale, np.sin(angle) * scale


def bf16(array):
    return np.asarray(array, np.float32).astype(ml_dtypes.bfloat16).astype(np.float32)


def analysis_depth(table):
    out = np.zeros((2, N, 2, 2, 2, M))
    for half in range(2):
        real, imag = table[:, :M], table[:, M:]
        out[half, :, 0, 0, half] = real
        out[half, :, 0, 1, half] = imag
        out[half, :, 1, 0, half] = imag
        out[half, :, 1, 1, half] = -real
    return bf16(out.reshape(2, N, 256))


def synthesis_depth(table):
    out = np.zeros((2, 2, M, 2, N))
    for half in range(2):
        out[:, half, :, half] = table.reshape(2, M, N)
    return bf16(out.reshape(128, 512))


def second_tables():
    cosine, sine = lateral_angles()
    out = np.zeros((8, 8, 4, 4, 2, 4, M))
    for block in range(8):
        rows = slice(block * M, (block + 1) * M)
        for x in range(4):
            out[block, :, :, x, 0, x] = cosine[:, rows].reshape(8, 4, M)
            out[block, :, :, x, 1, x] = sine[:, rows].reshape(8, 4, M)
    out = out.reshape(8, 128, 256)
    return bf16(out), bf16(out.transpose(0, 2, 1))


def first_tables():
    cosine, sine = lateral_angles()
    cos_x = cosine.T.reshape(M, 8, M)
    sin_x = sine.T.reshape(M, 8, M)
    forward = np.zeros((M, 2, 8, 2, 4, M))
    inverse = np.zeros((M, 2, 8, 2, 4, M))
    for j in range(4):
        forward[:, 0, :, 0, j] = cos_x
        forward[:, 0, :, 1, j] = -sin_x
        forward[:, 1, :, 0, j] = sin_x
        forward[:, 1, :, 1, j] = cos_x
        inverse[:, 0, :, 0, j] = cos_x
        inverse[:, 0, :, 1, j] = -sin_x
        inverse[:, 1, :, 0, j] = sin_x
        inverse[:, 1, :, 1, j] = cos_x
    return bf16(forward.reshape(512, 256)), bf16(inverse.reshape(512, 256))


def permutation(rows, lanes, sizes):
    total = int(np.prod([sizes[d] for d in rows]))
    position = np.arange(total).reshape([sizes[d] for d in rows])
    order = position.transpose([rows.index(d) for d in lanes]).reshape(-1)
    out = np.zeros((total, total))
    out[order, np.arange(total)] = 1.0
    return bf16(out)


def dot(a, b):
    return jnp.dot(a, b, preferred_element_type=F32)


def dot_nt(a, b):
    return lax.dot_general(a, b, (((1,), (1,)), ((), ())), preferred_element_type=F32)


def dot_tn(a, b):
    return lax.dot_general(a, b, (((0,), (0,)), ((), ())), preferred_element_type=F32)


def params(limit=40):
    return pltpu.CompilerParams(vmem_limit_bytes=limit * MIB)


def cost(flops, bytes_accessed, transcendentals=0):
    return pl.CostEstimate(
        flops=flops, bytes_accessed=bytes_accessed, transcendentals=transcendentals
    )


def whole(shape):
    return pl.BlockSpec(shape, lambda t, n: (0,) * len(shape))


def own(shape):
    return pl.BlockSpec((None,) + shape, lambda t, n: (n[0],) + (0,) * len(shape))


def second_forward(planes_ref, table, out_ref, first, count):
    for c in range(0, count, 2):
        one = planes_ref[first + c]
        two = planes_ref[first + c + 1]
        stacked = jnp.concatenate(
            [
                jnp.concatenate([one[:, :128], two[:, :128]], axis=1),
                jnp.concatenate([one[:, 128:], two[:, 128:]], axis=1),
            ],
            axis=0,
        )
        got = dot(table, stacked).astype(BF)
        for q in range(2):
            out_ref[:, (c + q) * 16 : (c + q + 1) * 16, :] = got[
                :, q * 128 : (q + 1) * 128
            ].reshape(8, 16, 128)


PARTS = C * 16
PAIR = PARTS + 16
STEP = 4
STEPS = C // STEP
FIELD_ROWS = STEP * 16
CARRY_ROWS = FIELD_ROWS + 32


def in_hbm(*arrays):
    return [pltpu.with_memory_space_constraint(jnp.asarray(a), pltpu.HBM) for a in arrays]


def analyse_kernel(
    block_ref, field_ref, weight_ref, depth_ref, table_ref, perm_ref, out_ref, planes_ref, rows_ref
):
    del block_ref

    @pl.when(pl.program_id(0) == 0)
    def _():
        rows_ref[...] = jnp.zeros((4, 256, M), F32)

    low = field_ref[:, 0].reshape(STEP * 128, N)
    high = field_ref[:, 1].reshape(STEP * 128, N)
    planes = dot(low, depth_ref[0].astype(BF)) + dot(high, depth_ref[1].astype(BF))
    planes_ref[...] = planes.astype(BF).reshape(STEP, 128, N)
    second_forward(planes_ref, table_ref[...].astype(BF), out_ref, 0, STEP)
    got = jnp.zeros((128, 256), F32)
    for i in range(4):
        for q in range(8):
            rows_ref[i, q * CP : q * CP + C, :] = weight_ref[
                pl.ds(q * 4 * C + i, C, stride=4), :
            ]
        got = got + dot_nt(perm_ref[i].astype(BF), rows_ref[i].astype(BF))
    got = got.astype(BF)
    for b in range(2):
        out_ref[:, FIELD_ROWS + b * 16 : FIELD_ROWS + (b + 1) * 16, :] = got[
            :, b * 128 : (b + 1) * 128
        ].reshape(8, 16, 128)


def analyse(block, *operands):
    return pl.pallas_call(
        analyse_kernel,
        grid_spec=pltpu.PrefetchScalarGridSpec(
            num_scalar_prefetch=1,
            grid=(STEPS,),
            in_specs=[
                pl.BlockSpec((STEP, 2, 4, M, N), lambda t, n: (t, 0, 0, 0, 0)),
                pl.BlockSpec((32 * C, M), lambda t, n: (t, 0)),
                whole((2, N, 256)),
                own((128, 256)),
                whole((4, 128, M)),
            ],
            out_specs=pl.BlockSpec((8, CARRY_ROWS, 128), lambda t, n: (0, t, 0)),
            scratch_shapes=[pltpu.VMEM((STEP, 128, 256), BF), pltpu.VMEM((4, 256, M), F32)],
        ),
        out_shape=jax.ShapeDtypeStruct((8, STEPS * CARRY_ROWS, 128), BF),
        compiler_params=params(),
        cost_estimate=cost(2 * 20 * 256 * 256 * 256, 3 * MIB),
        name="analyse",
    )(block, *in_hbm(*operands))


def gather_kernel(stride, in_ref, perm_ref, out_ref, sum_ref, rows_ref, turned_ref):
    for t in range(STEPS):
        rows = slice(t * stride, t * stride + FIELD_ROWS)
        total = in_ref[0, rows].astype(F32)
        for source in range(1, 8):
            total = total + in_ref[source, rows].astype(F32)
        sum_ref[t * FIELD_ROWS : (t + 1) * FIELD_ROWS] = total
    sum_ref[C * 16 :] = jnp.zeros((64, 128), F32)
    rows_ref[...] = jnp.zeros((512, 128), F32)
    for x in range(4):
        for j in range(4):
            rows_ref[x * 128 + j * 32 : x * 128 + j * 32 + CP, :] = sum_ref[
                pl.ds(j * 4 + x, CP, stride=16), :
            ]
    got = dot_nt(perm_ref[...].astype(BF), rows_ref[...].astype(BF))
    for x in range(4):
        turned_ref[pl.ds(x, 128, stride=4), :] = got[:, x * 128 : (x + 1) * 128]
    out_ref[...] = turned_ref[...].astype(BF).reshape(32, 16, 128)


def gather(parts, perm, stride):
    return pl.pallas_call(
        functools.partial(gather_kernel, stride),
        out_shape=jax.ShapeDtypeStruct((32, 16, 128), BF),
        scratch_shapes=[
            pltpu.VMEM((C * 16 + 64, 128), F32),
            pltpu.VMEM((512, 128), F32),
            pltpu.VMEM((512, 128), F32),
        ],
        compiler_params=params(),
        cost_estimate=cost(2 * 128 * 128 * 512, MIB),
        name="gather",
    )(parts, perm)


def scatter_kernel(*refs):
    if len(refs) == 6:
        in_ref, perm_ref, pair_ref, out_ref, turned_ref, rows_ref = refs
        out_ref[:, PARTS:, :] = pair_ref[...]
    else:
        in_ref, perm_ref, out_ref, turned_ref, rows_ref = refs
    turned_ref[...] = in_ref[...].reshape(512, 128).astype(F32)
    for x in range(4):
        block = turned_ref[pl.ds(x, 128, stride=4), :].astype(BF)
        got = dot_tn(block, perm_ref[...].astype(BF))
        for j in range(4):
            rows_ref[pl.ds(j * 4 + x, CP, stride=16), :] = got[j * 32 : j * 32 + CP]
    value = rows_ref[0 : C * 16].astype(BF)
    for target in range(8):
        out_ref[target, :PARTS] = value


def scatter(lines, perm, *pair):
    return pl.pallas_call(
        scatter_kernel,
        out_shape=jax.ShapeDtypeStruct((8, PAIR if pair else PARTS, 128), BF),
        scratch_shapes=[
            pltpu.VMEM((512, 128), F32),
            pltpu.VMEM((CP * 16, 128), F32),
        ],
        compiler_params=params(),
        cost_estimate=cost(2 * 128 * 128 * 512, MIB),
        name="scatter",
    )(lines, perm, *pair)


def lane_group(shape):
    return lax.broadcasted_iota(jnp.int32, shape, 1) // M % 4


def to_modes(lines_ref, first_ref):
    got = dot_tn(lines_ref[...].reshape(512, 128), first_ref[...].astype(BF))
    group = lane_group((M, 256))
    out = jnp.zeros((M, 256), F32)
    for j in range(4):
        out = jnp.where(group == j, got[j * M : (j + 1) * M], out)
    return out[:, :128], out[:, 128:]


def from_modes(real, imag, inverse_ref, out_ref):
    both = jnp.concatenate([real, imag], axis=1)
    group = lane_group((M, 256))
    rows = [jnp.where(group == j, both, 0.0) for j in range(4)]
    stacked = jnp.concatenate(rows, axis=0).astype(BF)
    out_ref[...] = dot_nt(inverse_ref[...].astype(BF), stacked).astype(BF).reshape(32, 16, 128)


def weight_row(part, c):
    index = part * C + c
    return (index // 8) * 256 + (index % 8) * CP


def mix_kernel(lines_ref, weight_ref, first_ref, inverse_ref, out_ref, spectrum_ref):
    real, imag = to_modes(lines_ref, first_ref)
    spectrum_ref[0] = real
    spectrum_ref[1] = imag
    mixed_real = jnp.zeros((CP, 128), F32)
    mixed_imag = jnp.zeros((CP, 128), F32)
    for c in range(C):
        w0 = weight_ref[weight_row(0, c) : weight_row(0, c) + CP, :]
        w1 = weight_ref[weight_row(1, c) : weight_row(1, c) + CP, :]
        s0 = real[c : c + 1]
        s1 = imag[c : c + 1]
        mixed_real = mixed_real + s0 * w0 - s1 * w1
        mixed_imag = mixed_imag + s0 * w1 + s1 * w0
    pad = jnp.zeros((M - CP, 128), F32)
    from_modes(
        jnp.concatenate([mixed_real, pad]),
        jnp.concatenate([mixed_imag, pad]),
        inverse_ref,
        out_ref,
    )


def mix_back_kernel(
    lines_ref, weight_ref, first_ref, inverse_ref, spectrum_ref, perm_ref, out_ref, pair_ref, acc_ref
):
    real, imag = to_modes(lines_ref, first_ref)
    both = jnp.concatenate([spectrum_ref[0], spectrum_ref[1], real, imag], axis=0)
    pair_ref[...] = dot_nt(perm_ref[...].astype(BF), both.astype(BF)).astype(BF).reshape(8, 16, 128)
    r0 = real[:CP]
    r1 = imag[:CP]
    acc_ref[...] = jnp.zeros((2, M, 128), F32)
    for c in range(C):
        w0 = weight_ref[weight_row(0, c) : weight_row(0, c) + CP, :]
        w1 = weight_ref[weight_row(1, c) : weight_row(1, c) + CP, :]
        acc_ref[0, c : c + 1, :] = jnp.sum(r0 * w0 + r1 * w1, axis=0, keepdims=True)
        acc_ref[1, c : c + 1, :] = jnp.sum(r1 * w0 - r0 * w1, axis=0, keepdims=True)
    from_modes(acc_ref[0], acc_ref[1], inverse_ref, out_ref)


def mix(lines, weight, first, inverse):
    return pl.pallas_call(
        mix_kernel,
        out_shape=[
            jax.ShapeDtypeStruct((32, 16, 128), BF),
            jax.ShapeDtypeStruct((2, M, 128), F32),
        ],
        compiler_params=params(),
        cost_estimate=cost(4 * 512 * 128 * 256, 2 * MIB),
        name="mix",
    )(lines, weight, first, inverse)


def mix_back(lines, weight, first, inverse, spectrum, perm):
    return pl.pallas_call(
        mix_back_kernel,
        out_shape=[
            jax.ShapeDtypeStruct((32, 16, 128), BF),
            jax.ShapeDtypeStruct((8, 16, 128), BF),
        ],
        scratch_shapes=[pltpu.VMEM((2, M, 128), F32)],
        compiler_params=params(),
        cost_estimate=cost(4 * 512 * 128 * 256, 2 * MIB),
        name="mix_back",
    )(lines, weight, first, inverse, spectrum, perm)


def weight_in_kernel(in_ref, perm_ref, out_ref):
    perm = perm_ref[...].astype(BF)
    for b in range(2):
        start = FIELD_ROWS + b * 16
        rows = in_ref[:, start : start + 16, :].reshape(128, 128)
        out_ref[b * 128 : (b + 1) * 128] = dot_tn(rows, perm)


def weight_in(parts, perm):
    return pl.pallas_call(
        weight_in_kernel,
        grid=(STEPS,),
        in_specs=[
            pl.BlockSpec((8, CARRY_ROWS, 128), lambda t: (0, t, 0)),
            pl.BlockSpec((128, 128), lambda t: (0, 0)),
        ],
        out_specs=pl.BlockSpec((256, 128), lambda t: (t, 0)),
        out_shape=jax.ShapeDtypeStruct((STEPS * 256, 128), F32),
        compiler_params=params(),
        cost_estimate=cost(2 * 128 * 128 * 1280, MIB),
        name="weight_in",
    )(parts, perm)


def second_inverse(in_ref, table_ref, planes_ref):
    table = table_ref[...].astype(BF)
    lane = lax.broadcasted_iota(jnp.int32, (128, 256), 1) % 128
    for c in range(0, C, 2):
        both = jnp.concatenate(
            [in_ref[:, (c + q) * 16 : (c + q + 1) * 16, :].reshape(128, 128) for q in range(2)],
            axis=1,
        )
        got = dot(table, both)
        for q in range(2):
            cos_part = got[:128, q * 128 : (q + 1) * 128]
            sin_part = got[128:, q * 128 : (q + 1) * 128]
            turned = pltpu.roll(sin_part, 64, 1)
            value = jnp.where(lane[:, :128] < 64, cos_part - turned, cos_part + turned)
            planes_ref[c + q] = value.astype(BF)


GRID_BLOCK = (C, 2, None, 16, N)
GRID = (C, 2, 4, M, N)


def grid_spec():
    return pl.BlockSpec(GRID_BLOCK, lambda t, *n: (0, 0, t // 2, t % 2, 0))


def widen(local_ref, spread_ref, same_ref, transposed):
    spread = spread_ref[...].astype(BF)
    multiply = dot_nt if transposed else dot
    rows = multiply(spread, local_ref[...]).astype(BF)
    return (dot_nt(rows, spread) * same_ref[...]).astype(BF)


def channels_kernel(transposed, field_ref, local_ref, spread_ref, same_ref, *refs):
    out_ref, wide_ref = refs[-2:]

    @pl.when(pl.program_id(0) == 0)
    def _():
        wide_ref[...] = widen(local_ref, spread_ref, same_ref, transposed)

    for x in range(2):
        value = dot(wide_ref[...], field_ref[:, x].reshape(C * 16, N)).reshape(C, 16, N)
        if not transposed:
            value = value + refs[0][...]
        out_ref[:, x] = value.astype(BF)


def channels(field, transposed, *operands):
    def block(shape):
        return pl.BlockSpec(shape, lambda t: (0,) * len(shape))

    shapes = [(C, C), (C * 16, C), (C * 16, C * 16), (C, 1, N)]
    return pl.pallas_call(
        functools.partial(channels_kernel, transposed),
        grid=(8,),
        in_specs=[grid_spec()] + [block(s) for s in shapes[: len(operands)]],
        out_specs=grid_spec(),
        out_shape=jax.ShapeDtypeStruct(GRID, BF),
        scratch_shapes=[pltpu.VMEM((C * 16, C * 16), BF)],
        compiler_params=params(16),
        cost_estimate=cost(2 * 10**9, 6 * MIB),
        name="channels",
    )(field, *in_hbm(*operands))


def local_kernel(
    block_ref,
    parts_ref,
    mixed_ref,
    cotangent_ref,
    inverse_ref,
    synth_ref,
    depth_ref,
    table_ref,
    activated_ref,
    slope_ref,
    out_ref,
    planes_ref,
    turned_ref,
    synth_scratch,
    depth_scratch,
):
    del block_ref
    step = pl.program_id(0)

    @pl.when(step == 0)
    def _():
        synth_scratch[...] = synth_ref[...].astype(BF)
        depth_scratch[...] = depth_ref[...].reshape(2 * N, 256).astype(BF)
        second_inverse(parts_ref, inverse_ref, planes_ref)

    rows = pl.ds(pl.multiple_of(step * 16, 16), 16)
    planes = planes_ref[:, rows, :].reshape(C * 16, 128)
    spatial = dot(planes, synth_scratch[...])
    slopes = []
    scale = 0.7978845608028654
    cubic = scale * 0.044715
    for x in range(2):
        pieces = []
        for c in range(C):
            value = spatial[c * 16 : (c + 1) * 16, x * N : (x + 1) * N]
            value = value + mixed_ref[c, x].astype(F32)
            square = value * value
            tanh = jnp.tanh(value * (scale + cubic * square))
            half = 0.5 + 0.5 * tanh
            activated_ref[c, x] = (value * half).astype(BF)
            d_inner = (0.5 * scale) + (1.5 * cubic) * square
            d_gelu = half + value * ((1.0 - tanh * tanh) * d_inner)
            slope = (cotangent_ref[c, x].astype(F32) * d_gelu).astype(BF)
            slope_ref[c, x] = slope
            pieces.append(slope)
        slopes.append(jnp.concatenate(pieces, axis=0))
    response = dot(jnp.concatenate(slopes, axis=1), depth_scratch[...])
    turned_ref[:, rows, :] = response.astype(BF).reshape(C, 16, 256)

    @pl.when(step == pl.num_programs(0) - 1)
    def _():
        second_forward(turned_ref, table_ref[...].astype(BF), out_ref, 0, C)


def local(block, parts, mixed, *operands):
    grid_shape = jax.ShapeDtypeStruct(GRID, BF)
    return pl.pallas_call(
        local_kernel,
        grid_spec=pltpu.PrefetchScalarGridSpec(
            num_scalar_prefetch=1,
            grid=(8,),
            in_specs=[
                whole((8, PARTS, 128)),
                grid_spec(),
                grid_spec(),
                own((256, 128)),
                whole((128, 512)),
                whole((2, N, 256)),
                own((128, 256)),
            ],
            out_specs=[grid_spec(), grid_spec(), whole((8, PARTS, 128))],
            scratch_shapes=[
                pltpu.VMEM((C, 128, 128), BF),
                pltpu.VMEM((C, 128, 256), BF),
                pltpu.VMEM((128, 512), BF),
                pltpu.VMEM((2 * N, 256), BF),
            ],
        ),
        out_shape=[grid_shape, grid_shape, jax.ShapeDtypeStruct((8, PARTS, 128), BF)],
        compiler_params=params(),
        cost_estimate=cost(10**9, 12 * MIB, 1310720),
        name="local",
    )(block, parts, mixed, *in_hbm(*operands))


def local_back_kernel(
    block_ref,
    parts_ref,
    mixed_ref,
    inverse_ref,
    synth_ref,
    perm_ref,
    out_ref,
    grad_ref,
    planes_ref,
    modes_ref,
    synth_scratch,
):
    del block_ref
    step = pl.program_id(0)

    @pl.when(step == 0)
    def _():
        synth_scratch[...] = synth_ref[...].astype(BF)
        second_inverse(parts_ref, inverse_ref, planes_ref)
        pair = parts_ref[:, PARTS:, :].reshape(128, 128)
        for i in range(4):
            modes_ref[pl.ds(i, 128, stride=4), :] = dot_tn(pair, perm_ref[i].astype(BF))

    r0 = modes_ref[8 * M : 8 * M + 4 * C, :]
    r1 = modes_ref[12 * M : 12 * M + 4 * C, :]
    for q in range(5):
        c = step * 5 + q
        s0 = modes_ref[pl.ds(c * 4, 4), :]
        s1 = modes_ref[pl.ds(4 * M + c * 4, 4), :]
        s0 = jnp.concatenate([s0] * C, axis=0)
        s1 = jnp.concatenate([s1] * C, axis=0)
        grad_ref[0, q] = s0 * r0 + s1 * r1
        grad_ref[1, q] = s0 * r1 - s1 * r0

    for h in range(2):
        rows = pl.ds(pl.multiple_of(step * 32 + h * 16, 16), 16)
        planes = planes_ref[:, rows, :].reshape(C * 16, 128)
        spatial = dot(planes, synth_scratch[...])
        for x in range(2):
            for c in range(C):
                value = spatial[c * 16 : (c + 1) * 16, x * N : (x + 1) * N]
                value = value + mixed_ref[c, x, h * 16 : (h + 1) * 16].astype(F32)
                out_ref[c, x, h * 16 : (h + 1) * 16] = value.astype(BF)


def local_back(block, parts, mixed, *operands):
    rows = pl.BlockSpec((C, 2, None, M, N), lambda t, n: (0, 0, t, 0, 0))
    return pl.pallas_call(
        local_back_kernel,
        grid_spec=pltpu.PrefetchScalarGridSpec(
            num_scalar_prefetch=1,
            grid=(4,),
            in_specs=[
                whole((8, PAIR, 128)),
                rows,
                own((256, 128)),
                whole((128, 512)),
                whole((4, 128, M)),
            ],
            out_specs=[
                rows,
                pl.BlockSpec((2, 5, 4 * C, M), lambda t, n: (0, t, 0, 0)),
            ],
            scratch_shapes=[
                pltpu.VMEM((C, 128, 128), BF),
                pltpu.VMEM((512, M), F32),
                pltpu.VMEM((128, 512), BF),
            ],
        ),
        out_shape=[
            jax.ShapeDtypeStruct(GRID, BF),
            jax.ShapeDtypeStruct((2, C, 4 * C, M), F32),
        ],
        compiler_params=params(),
        cost_estimate=cost(2 * 10**9, 6 * MIB),
        name="local_back",
    )(block, parts, mixed, *in_hbm(*operands))


def exchange(value, axis):
    return lax.all_to_all(value, axis, split_axis=0, concat_axis=0, tiled=True)


def shards(field, cotangent, spectral_weight, local_weight, local_bias):
    forward, inverse = depth_tables()
    forward_b, inverse_b = analysis_depth(forward), analysis_depth(inverse.T)
    synth_f, synth_b = synthesis_depth(inverse), synthesis_depth(forward.T)
    second, second_back = second_tables()
    first, first_back = first_tables()
    block = lax.axis_index("narrow").astype(jnp.int32).reshape(1)

    sizes = {"s": 2, "p": 2, "k": 32, "J": 8, "j": 4, "i": 4}
    perm_line = permutation("ksp", "spk", sizes)
    perm_weight = permutation("Jji", "iJj", sizes)
    perm_modes = permutation("Jji", "jJi", sizes)
    spread = np.zeros((C * 16, C), np.float32)
    spread[np.arange(C * 16), np.arange(C * 16) // 16] = 1.0
    same = bf16(np.equal(np.arange(C * 16)[:, None] % 16, np.arange(C * 16)[None, :] % 16))
    bias = jnp.broadcast_to(local_bias[:, None, None], (C, 1, N))

    perm_grad = np.stack([perm_weight[:, i * M : (i + 1) * M] for i in range(4)])

    shape = field.shape
    grid_field = field.reshape(GRID)
    grid_cotangent = cotangent.reshape(GRID)

    weight = jnp.transpose(spectral_weight, (0, 1, 2, 3, 5, 4)).reshape(8 * C * C, M)
    parts = exchange(analyse(block, grid_field, weight, forward_b, second, perm_grad), "narrow")
    mixed = channels(*in_hbm(grid_field), False, local_weight, spread, same, bias)
    weight = weight_in(parts, perm_modes)
    lines = exchange(gather(parts, perm_line, CARRY_ROWS), "wide")
    lines, spectrum = mix(lines, weight, first, first_back)
    lines = exchange(lines, "wide")
    parts = exchange(scatter(lines, perm_line), "narrow")
    activated, slope, parts = local(
        block, parts, mixed, grid_cotangent, second_back, synth_f, inverse_b, second
    )
    parts = exchange(parts, "narrow")
    mixed = channels(slope, True, local_weight, spread, same)
    lines = exchange(gather(parts, perm_line, FIELD_ROWS), "wide")
    lines, pair = mix_back(lines, weight, first, first_back, spectrum, perm_modes)
    lines = exchange(lines, "wide")
    parts = exchange(scatter(lines, perm_line, pair), "narrow")
    field_grad, weight_grad = local_back(block, parts, mixed, second_back, synth_b, perm_grad)
    return (
        activated.reshape(shape),
        field_grad.reshape(shape),
        weight_grad.reshape(spectral_weight.shape),
    )


def solution(mesh):
    return jax.shard_map(
        shards,
        mesh=mesh,
        in_specs=(
            P(None, "wide", "narrow", None),
            P(None, "wide", "narrow", None),
            P(None, None, None, "narrow", None, "wide"),
            P(),
            P(),
        ),
        out_specs=(
            P(None, "wide", "narrow", None),
            P(None, "wide", "narrow", None),
            P(None, None, None, "narrow", None, "wide"),
        ),
        check_vma=False,
    )
```

```python
import functools
import math

import jax
import jax.numpy as jnp
import ml_dtypes
import numpy as np
from jax import lax
from jax.experimental import pallas as pl
from jax.experimental.pallas import tpu as pltpu
from jax.sharding import PartitionSpec as P

N = 256
M = 32
C = 20
CP = 24
BF = jnp.bfloat16
F32 = jnp.float32
MIB = 1024 * 1024


def depth_tables():
    index = np.arange(N)
    freq = np.arange(M)
    angle = (2.0 * math.pi / N) * ((freq[:, None] * index[None, :]) % N)
    scale = 1.0 / math.sqrt(N)
    weights = np.where(freq == 0, 1.0, 2.0)[:, None]
    forward = (np.concatenate([np.cos(angle), -np.sin(angle)]) * scale).T
    inverse = np.concatenate([weights * np.cos(angle), -weights * np.sin(angle)]) * scale
    return forward, inverse


def lateral_angles():
    index = np.arange(N)
    base = np.arange(M)
    freq = np.where(base < M // 2, base, N - M + base)
    angle = (2.0 * math.pi / N) * ((freq[:, None] * index[None, :]) % N)
    scale = 1.0 / math.sqrt(N)
    return np.cos(angle) * scale, np.sin(angle) * scale


def bf16(array):
    return np.asarray(array, np.float32).astype(ml_dtypes.bfloat16).astype(np.float32)


def analysis_depth(table):
    out = np.zeros((N, 2, 2, 2, M))
    real, imag = table[:, :M], table[:, M:]
    out[:, 0, 0, 0] = real
    out[:, 0, 1, 0] = imag
    out[:, 1, 0, 0] = imag
    out[:, 1, 1, 0] = -real
    return bf16(out.reshape(N, 256))


def spread_depth(table):
    return jnp.concatenate([table, pltpu.roll(table, M, 1)], axis=0).astype(BF)


def spread_synth(table):
    zero = jnp.zeros((M, N), F32)
    rows = []
    for part in range(2):
        piece = table[part * M : (part + 1) * M]
        rows.append(jnp.concatenate([piece, zero], axis=1))
        rows.append(jnp.concatenate([zero, piece], axis=1))
    return jnp.concatenate(rows, axis=0).astype(BF)


def second_tables():
    cosine, sine = lateral_angles()
    out = np.zeros((8, 8, 4, 4, 2, 4, M))
    for block in range(8):
        rows = slice(block * M, (block + 1) * M)
        for x in range(4):
            out[block, :, :, x, 0, x] = cosine[:, rows].reshape(8, 4, M)
            out[block, :, :, x, 1, x] = sine[:, rows].reshape(8, 4, M)
    out = out.reshape(8, 128, 256)
    return bf16(out), bf16(out.transpose(0, 2, 1))


def first_table():
    cosine, sine = lateral_angles()
    cos_x = cosine.T.reshape(M, 8, M).transpose(1, 0, 2)
    sin_x = sine.T.reshape(M, 8, M).transpose(1, 0, 2)
    out = np.zeros((8, M, 2, 2, 4, M))
    for j in range(4):
        out[:, :, 0, 0, j] = cos_x
        out[:, :, 0, 1, j] = -sin_x
        out[:, :, 1, 0, j] = sin_x
        out[:, :, 1, 1, j] = cos_x
    return bf16(out.reshape(512, 256))


def line_table():
    out = np.zeros((M, 2, 2, 2, 2, M))
    for k in range(M):
        for part in range(2):
            for x in range(2):
                out[k, part, x, part, x, k] = 1.0
    return bf16(out.reshape(64, 256))


def permutation(rows, lanes, sizes):
    total = int(np.prod([sizes[d] for d in rows]))
    position = np.arange(total).reshape([sizes[d] for d in rows])
    order = position.transpose([rows.index(d) for d in lanes]).reshape(-1)
    out = np.zeros((total, total))
    out[order, np.arange(total)] = 1.0
    return bf16(out)


def dot(a, b):
    return jnp.dot(a, b, preferred_element_type=F32)


def dot_nt(a, b):
    return lax.dot_general(a, b, (((1,), (1,)), ((), ())), preferred_element_type=F32)


def dot_tn(a, b):
    return lax.dot_general(a, b, (((0,), (0,)), ((), ())), preferred_element_type=F32)


def params(limit=40):
    return pltpu.CompilerParams(vmem_limit_bytes=limit * MIB)


def cost(flops, bytes_accessed, transcendentals=0):
    return pl.CostEstimate(
        flops=flops, bytes_accessed=bytes_accessed, transcendentals=transcendentals
    )


def whole(shape):
    return pl.BlockSpec(shape, lambda t, n: (0,) * len(shape))


def own(shape):
    return pl.BlockSpec((None,) + shape, lambda t, n: (n[0],) + (0,) * len(shape))


def second_forward(planes_ref, table, out_ref, first, count):
    for c in range(0, count, 2):
        one = planes_ref[first + c]
        two = planes_ref[first + c + 1]
        stacked = jnp.concatenate(
            [
                jnp.concatenate([one[:, :128], two[:, :128]], axis=1),
                jnp.concatenate([one[:, 128:], two[:, 128:]], axis=1),
            ],
            axis=0,
        )
        got = dot(table, stacked).astype(BF)
        for q in range(2):
            out_ref[:, (c + q) * 16 : (c + q + 1) * 16, :] = got[
                :, q * 128 : (q + 1) * 128
            ].reshape(8, 16, 128)


PARTS = C * 16
PAIR = PARTS + 16
STEP = 4
STEPS = C // STEP
FIELD_ROWS = STEP * 16
CARRY_ROWS = FIELD_ROWS + 32


def in_hbm(*arrays):
    return [pltpu.with_memory_space_constraint(jnp.asarray(a), pltpu.HBM) for a in arrays]


def analyse_kernel(
    block_ref,
    field_ref,
    weight_ref,
    depth_ref,
    table_ref,
    perm_ref,
    out_ref,
    planes_ref,
    rows_ref,
    depth_scratch,
):
    del block_ref

    @pl.when(pl.program_id(0) == 0)
    def _():
        rows_ref[...] = jnp.zeros((4, 256, M), F32)
        depth_scratch[...] = spread_depth(depth_ref[...])

    rows = jnp.concatenate([field_ref[:, x].reshape(STEP * 128, N) for x in range(2)], axis=1)
    planes_ref[...] = dot(rows, depth_scratch[...]).astype(BF).reshape(STEP, 128, N)
    second_forward(planes_ref, table_ref[...].astype(BF), out_ref, 0, STEP)
    got = jnp.zeros((128, 256), F32)
    for i in range(4):
        for q in range(8):
            rows_ref[i, q * CP : q * CP + C, :] = weight_ref[
                pl.ds(q * 4 * C + i, C, stride=4), :
            ]
        got = got + dot_nt(perm_ref[i].astype(BF), rows_ref[i].astype(BF))
    got = got.astype(BF)
    for b in range(2):
        out_ref[:, FIELD_ROWS + b * 16 : FIELD_ROWS + (b + 1) * 16, :] = got[
            :, b * 128 : (b + 1) * 128
        ].reshape(8, 16, 128)


def analyse(block, *operands):
    return pl.pallas_call(
        analyse_kernel,
        grid_spec=pltpu.PrefetchScalarGridSpec(
            num_scalar_prefetch=1,
            grid=(STEPS,),
            in_specs=[
                pl.BlockSpec((STEP, 2, 4, M, N), lambda t, n: (t, 0, 0, 0, 0)),
                pl.BlockSpec((32 * C, M), lambda t, n: (t, 0)),
                whole((N, 256)),
                own((128, 256)),
                whole((4, 128, M)),
            ],
            out_specs=pl.BlockSpec((8, CARRY_ROWS, 128), lambda t, n: (0, t, 0)),
            scratch_shapes=[
                pltpu.VMEM((STEP, 128, 256), BF),
                pltpu.VMEM((4, 256, M), F32),
                pltpu.VMEM((2 * N, 256), BF),
            ],
        ),
        out_shape=jax.ShapeDtypeStruct((8, STEPS * CARRY_ROWS, 128), BF),
        compiler_params=params(),
        cost_estimate=cost(2 * 20 * 256 * 256 * 256, 3 * MIB),
        name="analyse",
    )(block, *in_hbm(*operands))


def gather_kernel(stride, in_ref, perm_ref, out_ref, sum_ref, rows_ref):
    for t in range(STEPS):
        rows = slice(t * stride, t * stride + FIELD_ROWS)
        total = in_ref[0, rows].astype(F32)
        for source in range(1, 8):
            total = total + in_ref[source, rows].astype(F32)
        sum_ref[t * FIELD_ROWS : (t + 1) * FIELD_ROWS] = total
    rows_ref[...] = jnp.zeros((640, 256), BF)
    for x in range(4):
        rows = sum_ref[pl.ds(x, 80, stride=4), :].astype(BF)
        rows_ref[x * 80 : (x + 1) * 80, :128] = rows
        rows_ref[320 + x * 80 : 320 + (x + 1) * 80, 128:] = rows
    got = dot_nt(perm_ref[...].astype(BF), rows_ref[...])
    out_ref[...] = got.astype(BF).reshape(32, 2, 640)


def gather(parts, perm, stride):
    return pl.pallas_call(
        functools.partial(gather_kernel, stride),
        out_shape=jax.ShapeDtypeStruct((32, 2, 640), BF),
        scratch_shapes=[pltpu.VMEM((PARTS, 128), F32), pltpu.VMEM((640, 256), BF)],
        compiler_params=params(),
        cost_estimate=cost(2 * 128 * 128 * 512, MIB),
        name="gather",
    )(parts, perm)


def scatter_kernel(*refs):
    if len(refs) == 5:
        in_ref, perm_ref, pair_ref, out_ref, rows_ref = refs
        out_ref[:, PARTS:, :] = pair_ref[...]
    else:
        in_ref, perm_ref, out_ref, rows_ref = refs
    got = dot_tn(in_ref[...].reshape(64, 640), perm_ref[...].astype(BF))
    for x in range(4):
        rows_ref[pl.ds(x, 80, stride=4), :] = (
            got[x * 80 : (x + 1) * 80, :128] + got[320 + x * 80 : 320 + (x + 1) * 80, 128:]
        )
    value = rows_ref[...].astype(BF)
    for target in range(8):
        out_ref[target, :PARTS] = value


def scatter(lines, perm, *pair):
    return pl.pallas_call(
        scatter_kernel,
        out_shape=jax.ShapeDtypeStruct((8, PAIR if pair else PARTS, 128), BF),
        scratch_shapes=[pltpu.VMEM((PARTS, 128), F32)],
        compiler_params=params(),
        cost_estimate=cost(2 * 128 * 128 * 512, MIB),
        name="scatter",
    )(lines, perm, *pair)


def lane_group(shape):
    return lax.broadcasted_iota(jnp.int32, shape, 1) // M % 4


def to_modes(lines_ref, first, rows_ref):
    lines = lines_ref[...].reshape(64, 640).astype(F32).T.astype(BF)
    got = jnp.zeros((80, 256), F32)
    for x in range(8):
        got = got + dot(lines[x * 80 : (x + 1) * 80], first[x * 64 : (x + 1) * 64])
    group = lane_group((CP, 128))
    both = []
    for part in range(2):
        rows_ref[part, 0:80] = got[:, part * 128 : (part + 1) * 128]
        rows_ref[part, 80:] = jnp.zeros((16, 128), F32)
        out = jnp.zeros((CP, 128), F32)
        for j in range(4):
            out = jnp.where(group == j, rows_ref[part, pl.ds(j, CP, stride=4), :], out)
        both.append(jnp.concatenate([out, jnp.zeros((M - CP, 128), F32)], axis=0))
    return both


def from_modes(real, imag, first, rows_ref, lines_ref, out_ref):
    group = lane_group((CP, 128))
    for j in range(4):
        rows_ref[0, pl.ds(j, CP, stride=4), :] = jnp.where(group == j, real, 0.0)
        rows_ref[1, pl.ds(j, CP, stride=4), :] = jnp.where(group == j, imag, 0.0)
    both = jnp.concatenate([rows_ref[0, 0:80], rows_ref[1, 0:80]], axis=1)
    got = dot_nt(first, both.astype(BF))
    for x in range(8):
        lines_ref[:, x * 80 : (x + 1) * 80] = got[x * 64 : (x + 1) * 64]
    out_ref[...] = lines_ref[...].astype(BF).reshape(32, 2, 640)


def weight_row(part, c):
    index = part * C + c
    return (index // 8) * 256 + (index % 8) * CP


def mix_kernel(lines_ref, weight_ref, first_ref, out_ref, spectrum_ref, rows_ref, turned_ref):
    first = first_ref[...].astype(BF)
    real, imag = to_modes(lines_ref, first, rows_ref)
    spectrum_ref[0] = real
    spectrum_ref[1] = imag
    mixed_real = jnp.zeros((CP, 128), F32)
    mixed_imag = jnp.zeros((CP, 128), F32)
    for c in range(C):
        w0 = weight_ref[weight_row(0, c) : weight_row(0, c) + CP, :]
        w1 = weight_ref[weight_row(1, c) : weight_row(1, c) + CP, :]
        s0 = real[c : c + 1]
        s1 = imag[c : c + 1]
        mixed_real = mixed_real + s0 * w0 - s1 * w1
        mixed_imag = mixed_imag + s0 * w1 + s1 * w0
    from_modes(mixed_real, mixed_imag, first, rows_ref, turned_ref, out_ref)


def mix_back_kernel(
    lines_ref,
    weight_ref,
    first_ref,
    spectrum_ref,
    perm_ref,
    out_ref,
    pair_ref,
    acc_ref,
    rows_ref,
    turned_ref,
):
    first = first_ref[...].astype(BF)
    real, imag = to_modes(lines_ref, first, rows_ref)
    both = jnp.concatenate([spectrum_ref[0], spectrum_ref[1], real, imag], axis=0)
    pair_ref[...] = dot_nt(perm_ref[...].astype(BF), both.astype(BF)).astype(BF).reshape(8, 16, 128)
    r0 = real[:CP]
    r1 = imag[:CP]
    acc_ref[...] = jnp.zeros((2, CP, 128), F32)
    for c in range(C):
        w0 = weight_ref[weight_row(0, c) : weight_row(0, c) + CP, :]
        w1 = weight_ref[weight_row(1, c) : weight_row(1, c) + CP, :]
        acc_ref[0, c : c + 1, :] = jnp.sum(r0 * w0 + r1 * w1, axis=0, keepdims=True)
        acc_ref[1, c : c + 1, :] = jnp.sum(r1 * w0 - r0 * w1, axis=0, keepdims=True)
    from_modes(acc_ref[0], acc_ref[1], first, rows_ref, turned_ref, out_ref)


def mix(*operands):
    return pl.pallas_call(
        mix_kernel,
        out_shape=[
            jax.ShapeDtypeStruct((32, 2, 640), BF),
            jax.ShapeDtypeStruct((2, M, 128), F32),
        ],
        scratch_shapes=[pltpu.VMEM((2, 4 * CP, 128), F32), pltpu.VMEM((64, 640), F32)],
        compiler_params=params(),
        cost_estimate=cost(4 * 512 * 128 * 256, 2 * MIB),
        name="mix",
    )(*operands)


def mix_back(*operands):
    return pl.pallas_call(
        mix_back_kernel,
        out_shape=[
            jax.ShapeDtypeStruct((32, 2, 640), BF),
            jax.ShapeDtypeStruct((8, 16, 128), BF),
        ],
        scratch_shapes=[
            pltpu.VMEM((2, CP, 128), F32),
            pltpu.VMEM((2, 4 * CP, 128), F32),
            pltpu.VMEM((64, 640), F32),
        ],
        compiler_params=params(),
        cost_estimate=cost(4 * 512 * 128 * 256, 2 * MIB),
        name="mix_back",
    )(*operands)


def weight_in_kernel(in_ref, perm_ref, out_ref):
    perm = perm_ref[...].astype(BF)
    for b in range(2):
        start = FIELD_ROWS + b * 16
        rows = in_ref[:, start : start + 16, :].reshape(128, 128)
        out_ref[b * 128 : (b + 1) * 128] = dot_tn(rows, perm)


def weight_in(parts, perm):
    return pl.pallas_call(
        weight_in_kernel,
        grid=(STEPS,),
        in_specs=[
            pl.BlockSpec((8, CARRY_ROWS, 128), lambda t: (0, t, 0)),
            pl.BlockSpec((128, 128), lambda t: (0, 0)),
        ],
        out_specs=pl.BlockSpec((256, 128), lambda t: (t, 0)),
        out_shape=jax.ShapeDtypeStruct((STEPS * 256, 128), F32),
        compiler_params=params(),
        cost_estimate=cost(2 * 128 * 128 * 1280, MIB),
        name="weight_in",
    )(parts, perm)


def second_inverse(in_ref, table, planes_ref):
    lane = lax.broadcasted_iota(jnp.int32, (128, 256), 1) % 128
    for c in range(0, C, 2):
        both = jnp.concatenate(
            [in_ref[:, (c + q) * 16 : (c + q + 1) * 16, :].reshape(128, 128) for q in range(2)],
            axis=1,
        )
        got = dot(table, both)
        for q in range(2):
            cos_part = got[:128, q * 128 : (q + 1) * 128]
            sin_part = got[128:, q * 128 : (q + 1) * 128]
            turned = pltpu.roll(sin_part, 64, 1)
            value = jnp.where(lane[:, :128] < 64, cos_part - turned, cos_part + turned)
            planes_ref[c + q] = value.astype(BF)


GRID_BLOCK = (C, 2, None, 16, N)
GRID = (C, 2, 4, M, N)


def grid_spec():
    return pl.BlockSpec(GRID_BLOCK, lambda t, *n: (0, 0, t // 2, t % 2, 0))


def widen(local_ref, spread_ref, same_ref, transposed):
    spread = spread_ref[...].astype(BF)
    multiply = dot_nt if transposed else dot
    rows = multiply(spread, local_ref[...]).astype(BF)
    return (dot_nt(rows, spread) * same_ref[...]).astype(BF)


def channels_kernel(transposed, *refs):
    if transposed:
        _, field_ref, local_ref, spread_ref, same_ref, synth_ref, out_ref, synth_out, wide_ref = refs
    else:
        (
            _,
            field_ref,
            local_ref,
            spread_ref,
            same_ref,
            bias_ref,
            synth_ref,
            depth_ref,
            table_ref,
            inverse_ref,
            out_ref,
            synth_out,
            depth_out,
            table_out,
            inverse_out,
            wide_ref,
        ) = refs

    @pl.when(pl.program_id(0) == 0)
    def _():
        wide_ref[...] = widen(local_ref, spread_ref, same_ref, transposed)
        synth_out[...] = spread_synth(synth_ref[...])
        if not transposed:
            depth_out[...] = spread_depth(depth_ref[...])
            table_out[...] = table_ref[...].astype(BF)
            inverse_out[...] = inverse_ref[...].astype(BF)

    for x in range(2):
        value = dot(wide_ref[...], field_ref[:, x].reshape(C * 16, N)).reshape(C, 16, N)
        if not transposed:
            value = value + bias_ref[...]
        out_ref[:, x] = value.astype(BF)


def channels(block, transposed, *operands):
    grid_shape = pltpu.HBM(GRID, BF)
    mixing = [whole((C, C)), whole((C * 16, C)), whole((C * 16, C * 16))]
    synth = whole((2 * M, N))
    synth_out = whole((128, 512))
    synth_shape = jax.ShapeDtypeStruct((128, 512), BF)
    if transposed:
        in_specs = [grid_spec()] + mixing + [synth]
        out_specs = [grid_spec(), synth_out]
        out_shape = [grid_shape, synth_shape]
    else:
        in_specs = [grid_spec()] + mixing + [whole((C, 1, N)), synth]
        in_specs += [whole((N, 256)), own((128, 256)), own((256, 128))]
        out_specs = [grid_spec(), synth_out]
        out_specs += [whole((2 * N, 256)), whole((128, 256)), whole((256, 128))]
        out_shape = [grid_shape, synth_shape] + [
            jax.ShapeDtypeStruct(s, BF) for s in ((2 * N, 256), (128, 256), (256, 128))
        ]
    return pl.pallas_call(
        functools.partial(channels_kernel, transposed),
        grid_spec=pltpu.PrefetchScalarGridSpec(
            num_scalar_prefetch=1,
            grid=(8,),
            in_specs=in_specs,
            out_specs=out_specs,
            scratch_shapes=[pltpu.VMEM((C * 16, C * 16), BF)],
        ),
        out_shape=out_shape,
        compiler_params=params(16),
        cost_estimate=cost(2 * 10**9, 6 * MIB),
        name="channels",
    )(block, *operands)


def piece(ref, t):
    return ref.at[:, :, t // 2, pl.ds(pl.multiple_of((t % 2) * 16, 16), 16), :]


def moving(source, target, t, sem):
    return pltpu.make_async_copy(piece(source, t), piece(target, t), sem.at[t])


def local_kernel(
    parts_ref,
    mixed_hbm,
    cotangent_hbm,
    synth_ref,
    depth_ref,
    table_ref,
    inverse_ref,
    activated_hbm,
    slope_hbm,
    out_ref,
    planes_ref,
    turned_ref,
    mixed_ref,
    cotangent_ref,
    activated_ref,
    slope_ref,
    mixed_sem,
    cotangent_sem,
    activated_sem,
    slope_sem,
):
    for t in range(8):
        moving(mixed_hbm, mixed_ref, t, mixed_sem).start()
        moving(cotangent_hbm, cotangent_ref, t, cotangent_sem).start()
    second_inverse(parts_ref, inverse_ref[...], planes_ref)
    scale = 0.7978845608028654
    cubic = scale * 0.044715

    def step(t, carry):
        moving(mixed_hbm, mixed_ref, t, mixed_sem).wait()
        moving(cotangent_hbm, cotangent_ref, t, cotangent_sem).wait()
        y = pl.ds(pl.multiple_of((t % 2) * 16, 16), 16)
        rows = pl.ds(pl.multiple_of(t * 16, 16), 16)
        planes = planes_ref[:, rows, :].reshape(C * 16, 128)
        spatial = dot(planes, synth_ref[...])
        slopes = []
        for x in range(2):
            pieces = []
            for c in range(C):
                value = spatial[c * 16 : (c + 1) * 16, x * N : (x + 1) * N]
                value = value + mixed_ref[c, x, t // 2, y, :].astype(F32)
                square = value * value
                tanh = jnp.tanh(value * (scale + cubic * square))
                half = 0.5 + 0.5 * tanh
                activated_ref[c, x, t // 2, y, :] = (value * half).astype(BF)
                d_inner = (0.5 * scale) + (1.5 * cubic) * square
                d_gelu = half + value * ((1.0 - tanh * tanh) * d_inner)
                slope = (cotangent_ref[c, x, t // 2, y, :].astype(F32) * d_gelu).astype(BF)
                slope_ref[c, x, t // 2, y, :] = slope
                pieces.append(slope)
            slopes.append(jnp.concatenate(pieces, axis=0))
        moving(activated_ref, activated_hbm, t, activated_sem).start()
        moving(slope_ref, slope_hbm, t, slope_sem).start()
        response = dot(jnp.concatenate(slopes, axis=1), depth_ref[...])
        turned_ref[:, rows, :] = response.astype(BF).reshape(C, 16, 256)
        return carry

    lax.fori_loop(0, 8, step, 0)
    second_forward(turned_ref, table_ref[...], out_ref, 0, C)
    for t in range(8):
        moving(activated_ref, activated_hbm, t, activated_sem).wait()
        moving(slope_ref, slope_hbm, t, slope_sem).wait()


VMEM = pl.BlockSpec(memory_space=pltpu.VMEM)
HBM = pl.BlockSpec(memory_space=pltpu.HBM)


def local(parts, mixed, cotangent, *tables):
    grid_shape = pltpu.HBM(GRID, BF)
    return pl.pallas_call(
        local_kernel,
        in_specs=[VMEM, HBM, HBM] + [VMEM] * len(tables),
        out_specs=[HBM, HBM, VMEM],
        out_shape=[grid_shape, grid_shape, jax.ShapeDtypeStruct((8, PARTS, 128), BF)],
        scratch_shapes=[pltpu.VMEM((C, 128, 128), BF), pltpu.VMEM((C, 128, 256), BF)]
        + [pltpu.VMEM(GRID, BF)] * 4
        + [pltpu.SemaphoreType.DMA((8,))] * 4,
        compiler_params=params(24),
        cost_estimate=cost(10**9, 12 * MIB, 1310720),
        name="local",
    )(parts, *in_hbm(mixed, cotangent), *tables)


def local_back_kernel(
    parts_ref,
    mixed_hbm,
    synth_ref,
    inverse_ref,
    perm_ref,
    out_hbm,
    grad_hbm,
    planes_ref,
    modes_ref,
    mixed_ref,
    out_ref,
    grad_ref,
    mixed_sem,
    out_sem,
    grad_sem,
):
    for t in range(8):
        moving(mixed_hbm, mixed_ref, t, mixed_sem).start()

    pair = parts_ref[:, PARTS:, :].reshape(128, 128)
    for i in range(4):
        modes_ref[pl.ds(i, 128, stride=4), :] = dot_tn(pair, perm_ref[i].astype(BF))
    r0 = modes_ref[8 * M : 8 * M + 4 * C, :]
    r1 = modes_ref[12 * M : 12 * M + 4 * C, :]

    def outer(t):
        return pltpu.make_async_copy(
            grad_ref.at[:, pl.ds(t * 5, 5)], grad_hbm.at[:, pl.ds(t * 5, 5)], grad_sem.at[t]
        )

    for c in range(C):
        s0 = jnp.concatenate([modes_ref[c * 4 : c * 4 + 4, :]] * C, axis=0)
        s1 = jnp.concatenate([modes_ref[4 * M + c * 4 : 4 * M + c * 4 + 4, :]] * C, axis=0)
        grad_ref[0, c] = s0 * r0 + s1 * r1
        grad_ref[1, c] = s0 * r1 - s1 * r0
        if c % 5 == 4:
            outer(c // 5).start()

    second_inverse(parts_ref, inverse_ref[...], planes_ref)

    def step(t, carry):
        moving(mixed_hbm, mixed_ref, t, mixed_sem).wait()
        y = pl.ds(pl.multiple_of((t % 2) * 16, 16), 16)
        rows = pl.ds(pl.multiple_of(t * 16, 16), 16)
        planes = planes_ref[:, rows, :].reshape(C * 16, 128)
        spatial = dot(planes, synth_ref[...])
        for x in range(2):
            for c in range(C):
                value = spatial[c * 16 : (c + 1) * 16, x * N : (x + 1) * N]
                value = value + mixed_ref[c, x, t // 2, y, :].astype(F32)
                out_ref[c, x, t // 2, y, :] = value.astype(BF)
        moving(out_ref, out_hbm, t, out_sem).start()
        return carry

    lax.fori_loop(0, 8, step, 0)
    for t in range(8):
        moving(out_ref, out_hbm, t, out_sem).wait()
    for t in range(4):
        outer(t).wait()


def local_back(parts, mixed, *tables):
    grad = (2, C, 4 * C, M)
    return pl.pallas_call(
        local_back_kernel,
        in_specs=[VMEM, HBM] + [VMEM] * len(tables),
        out_specs=[HBM, HBM],
        out_shape=[pltpu.HBM(GRID, BF), pltpu.HBM(grad, F32)],
        scratch_shapes=[
            pltpu.VMEM((C, 128, 128), BF),
            pltpu.VMEM((512, M), F32),
            pltpu.VMEM(GRID, BF),
            pltpu.VMEM(GRID, BF),
            pltpu.VMEM(grad, F32),
            pltpu.SemaphoreType.DMA((8,)),
            pltpu.SemaphoreType.DMA((8,)),
            pltpu.SemaphoreType.DMA((4,)),
        ],
        compiler_params=params(24),
        cost_estimate=cost(2 * 10**9, 6 * MIB),
        name="local_back",
    )(parts, *in_hbm(mixed), *tables)


def exchange(value, axis):
    return lax.all_to_all(value, axis, split_axis=0, concat_axis=0, tiled=True)


def shards(field, cotangent, spectral_weight, local_weight, local_bias):
    forward, inverse = depth_tables()
    forward_b, inverse_b = analysis_depth(forward), analysis_depth(inverse.T)
    synth_f, synth_b = bf16(inverse), bf16(forward.T)
    second, second_back = second_tables()
    first = first_table()
    block = lax.axis_index("narrow").astype(jnp.int32).reshape(1)

    sizes = {"J": 8, "j": 4, "i": 4}
    perm_line = line_table()
    perm_weight = permutation("Jji", "iJj", sizes)
    perm_modes = permutation("Jji", "jJi", sizes)
    spread = np.zeros((C * 16, C), np.float32)
    spread[np.arange(C * 16), np.arange(C * 16) // 16] = 1.0
    same = bf16(np.equal(np.arange(C * 16)[:, None] % 16, np.arange(C * 16)[None, :] % 16))
    bias = jnp.broadcast_to(local_bias[:, None, None], (C, 1, N))

    perm_grad = np.stack([perm_weight[:, i * M : (i + 1) * M] for i in range(4)])

    shape = field.shape
    grid_field = field.reshape(GRID)
    grid_cotangent = cotangent.reshape(GRID)

    weight = jnp.transpose(spectral_weight, (0, 1, 2, 3, 5, 4)).reshape(8 * C * C, M)
    parts = exchange(analyse(block, grid_field, weight, forward_b, second, perm_grad), "narrow")
    mixed, synth, depth, table, table_back = channels(
        block,
        False,
        *in_hbm(grid_field, local_weight, spread, same, bias),
        *in_hbm(synth_f, inverse_b, second, second_back),
    )
    weight = weight_in(parts, perm_modes)
    lines = exchange(gather(parts, perm_line, CARRY_ROWS), "wide")
    lines, spectrum = mix(lines, weight, first)
    lines = exchange(lines, "wide")
    parts = exchange(scatter(lines, perm_line), "narrow")
    activated, slope, parts = local(
        parts, mixed, grid_cotangent, synth, depth, table, table_back
    )
    parts = exchange(parts, "narrow")
    mixed, synth = channels(
        block, True, *in_hbm(slope, local_weight, spread, same, synth_b)
    )
    lines = exchange(gather(parts, perm_line, FIELD_ROWS), "wide")
    lines, pair = mix_back(lines, weight, first, spectrum, perm_modes)
    lines = exchange(lines, "wide")
    parts = exchange(scatter(lines, perm_line, pair), "narrow")
    field_grad, weight_grad = local_back(parts, mixed, synth, table_back, perm_grad)
    return (
        activated.reshape(shape),
        field_grad.reshape(shape),
        weight_grad.reshape(spectral_weight.shape),
    )


def solution(mesh):
    return jax.shard_map(
        shards,
        mesh=mesh,
        in_specs=(
            P(None, "wide", "narrow", None),
            P(None, "wide", "narrow", None),
            P(None, None, None, "narrow", None, "wide"),
            P(),
            P(),
        ),
        out_specs=(
            P(None, "wide", "narrow", None),
            P(None, "wide", "narrow", None),
            P(None, None, None, "narrow", None, "wide"),
        ),
        check_vma=False,
    )
```

```python
import functools
import math

import jax
import jax.numpy as jnp
import ml_dtypes
import numpy as np
from jax import lax
from jax.experimental import pallas as pl
from jax.experimental.pallas import tpu as pltpu
from jax.sharding import PartitionSpec as P

N = 256
M = 32
C = 20
CP = 24
BF = jnp.bfloat16
F32 = jnp.float32
MIB = 1024 * 1024


def depth_tables():
    index = np.arange(N)
    freq = np.arange(M)
    angle = (2.0 * math.pi / N) * ((freq[:, None] * index[None, :]) % N)
    scale = 1.0 / math.sqrt(N)
    weights = np.where(freq == 0, 1.0, 2.0)[:, None]
    forward = (np.concatenate([np.cos(angle), -np.sin(angle)]) * scale).T
    inverse = np.concatenate([weights * np.cos(angle), -weights * np.sin(angle)]) * scale
    return forward, inverse


def lateral_angles():
    index = np.arange(N)
    base = np.arange(M)
    freq = np.where(base < M // 2, base, N - M + base)
    angle = (2.0 * math.pi / N) * ((freq[:, None] * index[None, :]) % N)
    scale = 1.0 / math.sqrt(N)
    return np.cos(angle) * scale, np.sin(angle) * scale


def bf16(array):
    return np.asarray(array, np.float32).astype(ml_dtypes.bfloat16).astype(np.float32)


def analysis_depth(table):
    out = np.zeros((N, 2, 2, 2, M))
    real, imag = table[:, :M], table[:, M:]
    out[:, 0, 0, 0] = real
    out[:, 0, 1, 0] = imag
    out[:, 1, 0, 0] = imag
    out[:, 1, 1, 0] = -real
    return bf16(out.reshape(N, 256))


def spread_depth(table):
    return jnp.concatenate([table, pltpu.roll(table, M, 1)], axis=0).astype(BF)


def spread_synth(table):
    zero = jnp.zeros((M, N), F32)
    rows = []
    for part in range(2):
        piece = table[part * M : (part + 1) * M]
        rows.append(jnp.concatenate([piece, zero], axis=1))
        rows.append(jnp.concatenate([zero, piece], axis=1))
    return jnp.concatenate(rows, axis=0).astype(BF)


def second_tables():
    cosine, sine = lateral_angles()
    out = np.zeros((8, 8, 4, 4, 2, 4, M))
    for block in range(8):
        rows = slice(block * M, (block + 1) * M)
        for x in range(4):
            out[block, :, :, x, 0, x] = cosine[:, rows].reshape(8, 4, M)
            out[block, :, :, x, 1, x] = sine[:, rows].reshape(8, 4, M)
    out = out.reshape(8, 128, 256)
    return bf16(out), bf16(out.transpose(0, 2, 1))


def first_table():
    cosine, sine = lateral_angles()
    cos_x = cosine.T.reshape(M, 8, M).transpose(1, 0, 2)
    sin_x = sine.T.reshape(M, 8, M).transpose(1, 0, 2)
    out = np.zeros((8, M, 2, 2, 4, M))
    for j in range(4):
        out[:, :, 0, 0, j] = cos_x
        out[:, :, 0, 1, j] = -sin_x
        out[:, :, 1, 0, j] = sin_x
        out[:, :, 1, 1, j] = cos_x
    return bf16(out.reshape(512, 256))


def line_table():
    out = np.zeros((M, 2, 2, 2, 2, M))
    for k in range(M):
        for part in range(2):
            for x in range(2):
                out[k, part, x, part, x, k] = 1.0
    return bf16(out.reshape(64, 256))


def permutation(rows, lanes, sizes):
    total = int(np.prod([sizes[d] for d in rows]))
    position = np.arange(total).reshape([sizes[d] for d in rows])
    order = position.transpose([rows.index(d) for d in lanes]).reshape(-1)
    out = np.zeros((total, total))
    out[order, np.arange(total)] = 1.0
    return bf16(out)


def dot(a, b):
    return jnp.dot(a, b, preferred_element_type=F32)


def dot_nt(a, b):
    return lax.dot_general(a, b, (((1,), (1,)), ((), ())), preferred_element_type=F32)


def dot_tn(a, b):
    return lax.dot_general(a, b, (((0,), (0,)), ((), ())), preferred_element_type=F32)


def params(limit=40):
    return pltpu.CompilerParams(vmem_limit_bytes=limit * MIB)


def cost(flops, bytes_accessed, transcendentals=0):
    return pl.CostEstimate(
        flops=flops, bytes_accessed=bytes_accessed, transcendentals=transcendentals
    )


def whole(shape):
    return pl.BlockSpec(shape, lambda t, n: (0,) * len(shape))


def own(shape):
    return pl.BlockSpec((None,) + shape, lambda t, n: (n[0],) + (0,) * len(shape))


def second_forward(planes_ref, table, out_ref, first, count):
    for c in range(0, count, 2):
        one = planes_ref[first + c]
        two = planes_ref[first + c + 1]
        stacked = jnp.concatenate(
            [
                jnp.concatenate([one[:, :128], two[:, :128]], axis=1),
                jnp.concatenate([one[:, 128:], two[:, 128:]], axis=1),
            ],
            axis=0,
        )
        got = dot(table, stacked).astype(BF)
        for q in range(2):
            out_ref[:, (c + q) * 16 : (c + q + 1) * 16, :] = got[
                :, q * 128 : (q + 1) * 128
            ].reshape(8, 16, 128)


GRID = (C, 2, 4, M, N)
PARTS = C * 16
PAIR = PARTS + 16
STEP = 4
STEPS = C // STEP
FIELD_ROWS = STEP * 16
CARRY_ROWS = FIELD_ROWS + 32


VMEM = pl.BlockSpec(memory_space=pltpu.VMEM)
HBM = pl.BlockSpec(memory_space=pltpu.HBM)


def in_hbm(*arrays):
    return [pltpu.with_memory_space_constraint(jnp.asarray(a), pltpu.HBM) for a in arrays]


def analyse_kernel(
    block_ref,
    field_ref,
    weight_ref,
    depth_ref,
    table_ref,
    perm_ref,
    out_ref,
    planes_ref,
    rows_ref,
    depth_scratch,
):
    del block_ref

    @pl.when(pl.program_id(0) == 0)
    def _():
        rows_ref[...] = jnp.zeros((4, 256, M), F32)
        depth_scratch[...] = spread_depth(depth_ref[...])

    rows = jnp.concatenate([field_ref[:, x].reshape(STEP * 128, N) for x in range(2)], axis=1)
    planes_ref[...] = dot(rows, depth_scratch[...]).astype(BF).reshape(STEP, 128, N)
    second_forward(planes_ref, table_ref[...].astype(BF), out_ref, 0, STEP)
    got = jnp.zeros((128, 256), F32)
    for i in range(4):
        for q in range(8):
            rows_ref[i, q * CP : q * CP + C, :] = weight_ref[
                pl.ds(q * 4 * C + i, C, stride=4), :
            ]
        got = got + dot_nt(perm_ref[i].astype(BF), rows_ref[i].astype(BF))
    got = got.astype(BF)
    for b in range(2):
        out_ref[:, FIELD_ROWS + b * 16 : FIELD_ROWS + (b + 1) * 16, :] = got[
            :, b * 128 : (b + 1) * 128
        ].reshape(8, 16, 128)


def analyse(block, *operands):
    return pl.pallas_call(
        analyse_kernel,
        grid_spec=pltpu.PrefetchScalarGridSpec(
            num_scalar_prefetch=1,
            grid=(STEPS,),
            in_specs=[
                pl.BlockSpec((STEP, 2, 4, M, N), lambda t, n: (t, 0, 0, 0, 0)),
                pl.BlockSpec((32 * C, M), lambda t, n: (t, 0)),
                whole((N, 256)),
                own((128, 256)),
                whole((4, 128, M)),
            ],
            out_specs=pl.BlockSpec((8, CARRY_ROWS, 128), lambda t, n: (0, t, 0)),
            scratch_shapes=[
                pltpu.VMEM((STEP, 128, 256), BF),
                pltpu.VMEM((4, 256, M), F32),
                pltpu.VMEM((2 * N, 256), BF),
            ],
        ),
        out_shape=jax.ShapeDtypeStruct((8, STEPS * CARRY_ROWS, 128), BF),
        compiler_params=params(),
        cost_estimate=cost(2 * 20 * 256 * 256 * 256, 3 * MIB),
        name="analyse",
    )(block, *in_hbm(*operands))


def gather_kernel(stride, in_ref, perm_ref, out_ref, sum_ref, rows_ref):
    for t in range(STEPS):
        rows = slice(t * stride, t * stride + FIELD_ROWS)
        total = in_ref[0, rows].astype(F32)
        for source in range(1, 8):
            total = total + in_ref[source, rows].astype(F32)
        sum_ref[t * FIELD_ROWS : (t + 1) * FIELD_ROWS] = total
    rows_ref[...] = jnp.zeros((640, 256), BF)
    for x in range(4):
        rows = sum_ref[pl.ds(x, 80, stride=4), :].astype(BF)
        rows_ref[x * 80 : (x + 1) * 80, :128] = rows
        rows_ref[320 + x * 80 : 320 + (x + 1) * 80, 128:] = rows
    got = dot_nt(perm_ref[...].astype(BF), rows_ref[...])
    out_ref[...] = got.astype(BF).reshape(32, 2, 640)


def gather(parts, perm, stride):
    return pl.pallas_call(
        functools.partial(gather_kernel, stride),
        out_shape=jax.ShapeDtypeStruct((32, 2, 640), BF),
        scratch_shapes=[pltpu.VMEM((PARTS, 128), F32), pltpu.VMEM((640, 256), BF)],
        compiler_params=params(),
        cost_estimate=cost(2 * 128 * 128 * 512, MIB),
        name="gather",
    )(parts, perm)


def scatter_kernel(*refs):
    if len(refs) == 5:
        in_ref, perm_ref, pair_ref, out_ref, rows_ref = refs
        out_ref[:, PARTS:, :] = pair_ref[...]
    else:
        in_ref, perm_ref, out_ref, rows_ref = refs
    got = dot_tn(in_ref[...].reshape(64, 640), perm_ref[...].astype(BF))
    for x in range(4):
        rows_ref[pl.ds(x, 80, stride=4), :] = (
            got[x * 80 : (x + 1) * 80, :128] + got[320 + x * 80 : 320 + (x + 1) * 80, 128:]
        )
    value = rows_ref[...].astype(BF)
    for target in range(8):
        out_ref[target, :PARTS] = value


def scatter(lines, perm, *pair):
    return pl.pallas_call(
        scatter_kernel,
        out_shape=jax.ShapeDtypeStruct((8, PAIR if pair else PARTS, 128), BF),
        scratch_shapes=[pltpu.VMEM((PARTS, 128), F32)],
        compiler_params=params(),
        cost_estimate=cost(2 * 128 * 128 * 512, MIB),
        name="scatter",
    )(lines, perm, *pair)


def lane_group(shape):
    return lax.broadcasted_iota(jnp.int32, shape, 1) // M % 4


def to_modes(lines_ref, first, rows_ref):
    lines = lines_ref[...].reshape(64, 640).astype(F32).T.astype(BF)
    got = jnp.zeros((80, 256), F32)
    for x in range(8):
        got = got + dot(lines[x * 80 : (x + 1) * 80], first[x * 64 : (x + 1) * 64])
    group = lane_group((CP, 128))
    both = []
    for part in range(2):
        rows_ref[part, 0:80] = got[:, part * 128 : (part + 1) * 128]
        rows_ref[part, 80:] = jnp.zeros((16, 128), F32)
        out = jnp.zeros((CP, 128), F32)
        for j in range(4):
            out = jnp.where(group == j, rows_ref[part, pl.ds(j, CP, stride=4), :], out)
        both.append(jnp.concatenate([out, jnp.zeros((M - CP, 128), F32)], axis=0))
    return both


def from_modes(real, imag, first, rows_ref, lines_ref, out_ref):
    group = lane_group((CP, 128))
    for j in range(4):
        rows_ref[0, pl.ds(j, CP, stride=4), :] = jnp.where(group == j, real, 0.0)
        rows_ref[1, pl.ds(j, CP, stride=4), :] = jnp.where(group == j, imag, 0.0)
    both = jnp.concatenate([rows_ref[0, 0:80], rows_ref[1, 0:80]], axis=1)
    got = dot_nt(first, both.astype(BF))
    for x in range(8):
        lines_ref[:, x * 80 : (x + 1) * 80] = got[x * 64 : (x + 1) * 64]
    out_ref[...] = lines_ref[...].astype(BF).reshape(32, 2, 640)


def weight_row(part, c):
    index = part * C + c
    return (index // 8) * 256 + (index % 8) * CP


def mix_kernel(lines_ref, weight_ref, first_ref, out_ref, spectrum_ref, rows_ref, turned_ref):
    first = first_ref[...].astype(BF)
    real, imag = to_modes(lines_ref, first, rows_ref)
    spectrum_ref[0] = real
    spectrum_ref[1] = imag
    mixed_real = jnp.zeros((CP, 128), F32)
    mixed_imag = jnp.zeros((CP, 128), F32)
    for c in range(C):
        w0 = weight_ref[weight_row(0, c) : weight_row(0, c) + CP, :]
        w1 = weight_ref[weight_row(1, c) : weight_row(1, c) + CP, :]
        s0 = real[c : c + 1]
        s1 = imag[c : c + 1]
        mixed_real = mixed_real + s0 * w0 - s1 * w1
        mixed_imag = mixed_imag + s0 * w1 + s1 * w0
    from_modes(mixed_real, mixed_imag, first, rows_ref, turned_ref, out_ref)


def mix_back_kernel(
    lines_ref,
    weight_ref,
    first_ref,
    spectrum_ref,
    perm_ref,
    out_ref,
    pair_ref,
    acc_ref,
    rows_ref,
    turned_ref,
):
    first = first_ref[...].astype(BF)
    real, imag = to_modes(lines_ref, first, rows_ref)
    both = jnp.concatenate([spectrum_ref[0], spectrum_ref[1], real, imag], axis=0)
    pair_ref[...] = dot_nt(perm_ref[...].astype(BF), both.astype(BF)).astype(BF).reshape(8, 16, 128)
    r0 = real[:CP]
    r1 = imag[:CP]
    acc_ref[...] = jnp.zeros((2, CP, 128), F32)
    for c in range(C):
        w0 = weight_ref[weight_row(0, c) : weight_row(0, c) + CP, :]
        w1 = weight_ref[weight_row(1, c) : weight_row(1, c) + CP, :]
        acc_ref[0, c : c + 1, :] = jnp.sum(r0 * w0 + r1 * w1, axis=0, keepdims=True)
        acc_ref[1, c : c + 1, :] = jnp.sum(r1 * w0 - r0 * w1, axis=0, keepdims=True)
    from_modes(acc_ref[0], acc_ref[1], first, rows_ref, turned_ref, out_ref)


def mix(*operands):
    return pl.pallas_call(
        mix_kernel,
        out_shape=[
            jax.ShapeDtypeStruct((32, 2, 640), BF),
            jax.ShapeDtypeStruct((2, M, 128), F32),
        ],
        scratch_shapes=[pltpu.VMEM((2, 4 * CP, 128), F32), pltpu.VMEM((64, 640), F32)],
        compiler_params=params(),
        cost_estimate=cost(4 * 512 * 128 * 256, 2 * MIB),
        name="mix",
    )(*operands)


def mix_back(*operands):
    return pl.pallas_call(
        mix_back_kernel,
        out_shape=[
            jax.ShapeDtypeStruct((32, 2, 640), BF),
            jax.ShapeDtypeStruct((8, 16, 128), BF),
        ],
        scratch_shapes=[
            pltpu.VMEM((2, CP, 128), F32),
            pltpu.VMEM((2, 4 * CP, 128), F32),
            pltpu.VMEM((64, 640), F32),
        ],
        compiler_params=params(),
        cost_estimate=cost(4 * 512 * 128 * 256, 2 * MIB),
        name="mix_back",
    )(*operands)


def weight_in_kernel(
    block_ref,
    in_ref,
    perm_ref,
    synth_ref,
    depth_ref,
    table_ref,
    inverse_ref,
    back_ref,
    out_ref,
    synth_out,
    depth_out,
    table_out,
    inverse_out,
    back_out,
):
    del block_ref

    @pl.when(pl.program_id(0) == 0)
    def _():
        synth_out[...] = spread_synth(synth_ref[...])
        depth_out[...] = spread_depth(depth_ref[...])
        table_out[...] = table_ref[...].astype(BF)
        inverse_out[...] = inverse_ref[...].astype(BF)
        back_out[...] = spread_synth(back_ref[...])

    perm = perm_ref[...].astype(BF)
    for b in range(2):
        start = FIELD_ROWS + b * 16
        rows = in_ref[:, start : start + 16, :].reshape(128, 128)
        out_ref[b * 128 : (b + 1) * 128] = dot_tn(rows, perm)


def weight_in(block, parts, perm, *tables):
    shapes = [(128, 512), (2 * N, 256), (128, 256), (256, 128), (128, 512)]
    return pl.pallas_call(
        weight_in_kernel,
        grid_spec=pltpu.PrefetchScalarGridSpec(
            num_scalar_prefetch=1,
            grid=(STEPS,),
            in_specs=[
                pl.BlockSpec((8, CARRY_ROWS, 128), lambda t, n: (0, t, 0)),
                whole((128, 128)),
                whole((2 * M, N)),
                whole((N, 256)),
                own((128, 256)),
                own((256, 128)),
                whole((2 * M, N)),
            ],
            out_specs=[pl.BlockSpec((256, 128), lambda t, n: (t, 0))] + [whole(s) for s in shapes],
        ),
        out_shape=[jax.ShapeDtypeStruct((STEPS * 256, 128), F32)]
        + [jax.ShapeDtypeStruct(s, BF) for s in shapes],
        compiler_params=params(16),
        cost_estimate=cost(2 * 128 * 128 * 1280, 3 * MIB),
        name="weight_in",
    )(block, parts, *in_hbm(perm, *tables))


def second_inverse(in_ref, table, planes_ref):
    lane = lax.broadcasted_iota(jnp.int32, (128, 256), 1) % 128
    for c in range(0, C, 2):
        both = jnp.concatenate(
            [in_ref[:, (c + q) * 16 : (c + q + 1) * 16, :].reshape(128, 128) for q in range(2)],
            axis=1,
        )
        got = dot(table, both)
        for q in range(2):
            cos_part = got[:128, q * 128 : (q + 1) * 128]
            sin_part = got[128:, q * 128 : (q + 1) * 128]
            turned = pltpu.roll(sin_part, 64, 1)
            value = jnp.where(lane[:, :128] < 64, cos_part - turned, cos_part + turned)
            planes_ref[c + q] = value.astype(BF)


def piece(ref, t):
    return ref.at[:, :, t // 2, pl.ds(pl.multiple_of((t % 2) * 16, 16), 16), :]


def moving(source, target, t, sem):
    return pltpu.make_async_copy(piece(source, t), piece(target, t), sem.at[t])


def widen(local, transposed):
    row = lax.broadcasted_iota(jnp.int32, (C * 16, C), 0)
    channel = lax.broadcasted_iota(jnp.int32, (C * 16, C), 1)
    spread = jnp.where(row // 16 == channel, 1.0, 0.0).astype(BF)
    multiply = dot_nt if transposed else dot
    rows = multiply(spread, local).astype(BF)
    row = lax.broadcasted_iota(jnp.int32, (C * 16, C * 16), 0)
    lane = lax.broadcasted_iota(jnp.int32, (C * 16, C * 16), 1)
    return jnp.where(row % 16 == lane % 16, dot_nt(rows, spread), 0.0).astype(BF)


def local_kernel(
    parts_ref,
    field_hbm,
    cotangent_hbm,
    synth_ref,
    depth_ref,
    table_ref,
    inverse_ref,
    local_ref,
    bias_ref,
    activated_hbm,
    mixed_ref,
    out_ref,
    planes_ref,
    turned_ref,
    wide_ref,
    wide_back_ref,
    field_ref,
    cotangent_ref,
    activated_ref,
    field_sem,
    cotangent_sem,
    activated_sem,
):
    for t in range(8):
        moving(field_hbm, field_ref, t, field_sem).start()
        moving(cotangent_hbm, cotangent_ref, t, cotangent_sem).start()
    wide_ref[...] = widen(local_ref[...], False)
    wide_back_ref[...] = widen(local_ref[...], True)
    second_inverse(parts_ref, inverse_ref[...], planes_ref)
    scale = 0.7978845608028654
    cubic = scale * 0.044715

    def step(t, carry):
        moving(field_hbm, field_ref, t, field_sem).wait()
        moving(cotangent_hbm, cotangent_ref, t, cotangent_sem).wait()
        y = pl.ds(pl.multiple_of((t % 2) * 16, 16), 16)
        rows = pl.ds(pl.multiple_of(t * 16, 16), 16)
        planes = planes_ref[:, rows, :].reshape(C * 16, 128)
        left = jnp.concatenate([planes, wide_ref[...]], axis=1)
        slopes = []
        for x in range(2):
            field = field_ref[:, x, t // 2, y, :].reshape(C * 16, N)
            right = jnp.concatenate([synth_ref[:, x * N : (x + 1) * N], field], axis=0)
            values = dot(left, right)
            pieces = []
            for c in range(C):
                value = values[c * 16 : (c + 1) * 16] + bias_ref[c]
                square = value * value
                half = 0.5 + 0.5 * jnp.tanh(value * (scale + cubic * square))
                activated = value * half
                activated_ref[c, x, t // 2, y, :] = activated.astype(BF)
                d_inner = (2.0 * scale) + (6.0 * cubic) * square
                d_gelu = half + (activated * (1.0 - half)) * d_inner
                pieces.append((cotangent_ref[c, x, t // 2, y, :].astype(F32) * d_gelu).astype(BF))
            slope = jnp.concatenate(pieces, axis=0)
            slopes.append(slope)
            mixed = dot(wide_back_ref[...], slope).astype(BF)
            mixed_ref[:, x, t // 2, y, :] = mixed.reshape(C, 16, N)
        moving(activated_ref, activated_hbm, t, activated_sem).start()
        response = dot(jnp.concatenate(slopes, axis=1), depth_ref[...])
        turned_ref[:, rows, :] = response.astype(BF).reshape(C, 16, 256)
        return carry

    lax.fori_loop(0, 8, step, 0)
    second_forward(turned_ref, table_ref[...], out_ref, 0, C)
    for t in range(8):
        moving(activated_ref, activated_hbm, t, activated_sem).wait()


def local(parts, field, cotangent, *operands):
    return pl.pallas_call(
        local_kernel,
        in_specs=[VMEM, HBM, HBM] + [VMEM] * 5 + [pl.BlockSpec(memory_space=pltpu.SMEM)],
        out_specs=[HBM, VMEM, VMEM],
        out_shape=[
            pltpu.HBM(GRID, BF),
            jax.ShapeDtypeStruct(GRID, BF),
            jax.ShapeDtypeStruct((8, PARTS, 128), BF),
        ],
        scratch_shapes=[pltpu.VMEM((C, 128, 128), BF), pltpu.VMEM((C, 128, 256), BF)]
        + [pltpu.VMEM((C * 16, C * 16), BF)] * 2
        + [pltpu.VMEM(GRID, BF)] * 3
        + [pltpu.SemaphoreType.DMA((8,))] * 3,
        compiler_params=params(24),
        cost_estimate=cost(3 * 10**9, 12 * MIB, 1310720),
        name="local",
    )(parts, *in_hbm(field, cotangent), *operands)


def local_back_kernel(
    parts_ref,
    mixed_ref,
    synth_ref,
    inverse_ref,
    perm_ref,
    out_hbm,
    grad_hbm,
    planes_ref,
    modes_ref,
    out_ref,
    grad_ref,
    out_sem,
    grad_sem,
):
    pair = parts_ref[:, PARTS:, :].reshape(128, 128)
    for i in range(4):
        modes_ref[pl.ds(i, 128, stride=4), :] = dot_tn(pair, perm_ref[i].astype(BF))
    r0 = modes_ref[8 * M : 8 * M + 4 * C, :]
    r1 = modes_ref[12 * M : 12 * M + 4 * C, :]

    def outer(t):
        return pltpu.make_async_copy(
            grad_ref.at[:, pl.ds(t * 5, 5)], grad_hbm.at[:, pl.ds(t * 5, 5)], grad_sem.at[t]
        )

    for c in range(C):
        s0 = jnp.concatenate([modes_ref[c * 4 : c * 4 + 4, :]] * C, axis=0)
        s1 = jnp.concatenate([modes_ref[4 * M + c * 4 : 4 * M + c * 4 + 4, :]] * C, axis=0)
        grad_ref[0, c] = s0 * r0 + s1 * r1
        grad_ref[1, c] = s0 * r1 - s1 * r0
        if c % 5 == 4:
            outer(c // 5).start()

    second_inverse(parts_ref, inverse_ref[...], planes_ref)

    def step(t, carry):
        y = pl.ds(pl.multiple_of((t % 2) * 16, 16), 16)
        rows = pl.ds(pl.multiple_of(t * 16, 16), 16)
        planes = planes_ref[:, rows, :].reshape(C * 16, 128)
        spatial = dot(planes, synth_ref[...])
        for x in range(2):
            for c in range(C):
                value = spatial[c * 16 : (c + 1) * 16, x * N : (x + 1) * N]
                value = value + mixed_ref[c, x, t // 2, y, :].astype(F32)
                out_ref[c, x, t // 2, y, :] = value.astype(BF)
        moving(out_ref, out_hbm, t, out_sem).start()
        return carry

    lax.fori_loop(0, 8, step, 0)
    for t in range(8):
        moving(out_ref, out_hbm, t, out_sem).wait()
    for t in range(4):
        outer(t).wait()


def local_back(parts, mixed, *tables):
    grad = (2, C, 4 * C, M)
    return pl.pallas_call(
        local_back_kernel,
        in_specs=[VMEM] * (2 + len(tables)),
        out_specs=[HBM, HBM],
        out_shape=[pltpu.HBM(GRID, BF), pltpu.HBM(grad, F32)],
        scratch_shapes=[
            pltpu.VMEM((C, 128, 128), BF),
            pltpu.VMEM((512, M), F32),
            pltpu.VMEM(GRID, BF),
            pltpu.VMEM(grad, F32),
            pltpu.SemaphoreType.DMA((8,)),
            pltpu.SemaphoreType.DMA((4,)),
        ],
        compiler_params=params(24),
        cost_estimate=cost(2 * 10**9, 6 * MIB),
        name="local_back",
    )(parts, mixed, *tables)


def exchange(value, axis):
    return lax.all_to_all(value, axis, split_axis=0, concat_axis=0, tiled=True)


def shards(field, cotangent, spectral_weight, local_weight, local_bias):
    forward, inverse = depth_tables()
    forward_b, inverse_b = analysis_depth(forward), analysis_depth(inverse.T)
    synth_f, synth_b = bf16(inverse), bf16(forward.T)
    second, second_back = second_tables()
    first = first_table()
    block = lax.axis_index("narrow").astype(jnp.int32).reshape(1)

    sizes = {"J": 8, "j": 4, "i": 4}
    perm_line = line_table()
    perm_weight = permutation("Jji", "iJj", sizes)
    perm_modes = permutation("Jji", "jJi", sizes)
    perm_grad = np.stack([perm_weight[:, i * M : (i + 1) * M] for i in range(4)])

    shape = field.shape
    grid_field = field.reshape(GRID)
    grid_cotangent = cotangent.reshape(GRID)

    weight = jnp.transpose(spectral_weight, (0, 1, 2, 3, 5, 4)).reshape(8 * C * C, M)
    parts = exchange(analyse(block, grid_field, weight, forward_b, second, perm_grad), "narrow")
    weight, synth, depth, table, table_back, back = weight_in(
        block, parts, perm_modes, synth_f, inverse_b, second, second_back, synth_b
    )
    lines = exchange(gather(parts, perm_line, CARRY_ROWS), "wide")
    lines, spectrum = mix(lines, weight, first)
    lines = exchange(lines, "wide")
    parts = exchange(scatter(lines, perm_line), "narrow")
    activated, mixed, parts = local(
        parts,
        grid_field,
        grid_cotangent,
        synth,
        depth,
        table,
        table_back,
        local_weight,
        local_bias,
    )
    parts = exchange(parts, "narrow")
    lines = exchange(gather(parts, perm_line, FIELD_ROWS), "wide")
    lines, pair = mix_back(lines, weight, first, spectrum, perm_modes)
    lines = exchange(lines, "wide")
    parts = exchange(scatter(lines, perm_line, pair), "narrow")
    field_grad, weight_grad = local_back(parts, mixed, back, table_back, perm_grad)
    return (
        activated.reshape(shape),
        field_grad.reshape(shape),
        weight_grad.reshape(spectral_weight.shape),
    )


def solution(mesh):
    return jax.shard_map(
        shards,
        mesh=mesh,
        in_specs=(
            P(None, "wide", "narrow", None),
            P(None, "wide", "narrow", None),
            P(None, None, None, "narrow", None, "wide"),
            P(),
            P(),
        ),
        out_specs=(
            P(None, "wide", "narrow", None),
            P(None, "wide", "narrow", None),
            P(None, None, None, "narrow", None, "wide"),
        ),
        check_vma=False,
    )
```

```python
import functools
import math

import jax
import jax.numpy as jnp
import ml_dtypes
import numpy as np
from jax import lax
from jax.experimental import pallas as pl
from jax.experimental.pallas import tpu as pltpu
from jax.sharding import PartitionSpec as P

N = 256
M = 32
C = 20
CP = 24
BF = jnp.bfloat16
F32 = jnp.float32
MIB = 1024 * 1024


def depth_tables():
    index = np.arange(N)
    freq = np.arange(M)
    angle = (2.0 * math.pi / N) * ((freq[:, None] * index[None, :]) % N)
    scale = 1.0 / math.sqrt(N)
    weights = np.where(freq == 0, 1.0, 2.0)[:, None]
    forward = (np.concatenate([np.cos(angle), -np.sin(angle)]) * scale).T
    inverse = np.concatenate([weights * np.cos(angle), -weights * np.sin(angle)]) * scale
    return forward, inverse


def lateral_angles():
    index = np.arange(N)
    base = np.arange(M)
    freq = np.where(base < M // 2, base, N - M + base)
    angle = (2.0 * math.pi / N) * ((freq[:, None] * index[None, :]) % N)
    scale = 1.0 / math.sqrt(N)
    return np.cos(angle) * scale, np.sin(angle) * scale


def bf16(array):
    return np.asarray(array, np.float32).astype(ml_dtypes.bfloat16).astype(np.float32)


def analysis_depth(table):
    out = np.zeros((N, 2, 2, 2, M))
    real, imag = table[:, :M], table[:, M:]
    out[:, 0, 0, 0] = real
    out[:, 0, 1, 0] = imag
    out[:, 1, 0, 0] = imag
    out[:, 1, 1, 0] = -real
    return bf16(out.reshape(N, 256))


def spread_depth(table):
    return jnp.concatenate([table, pltpu.roll(table, M, 1)], axis=0).astype(BF)


def spread_synth(table):
    zero = jnp.zeros((M, N), F32)
    rows = []
    for part in range(2):
        piece = table[part * M : (part + 1) * M]
        rows.append(jnp.concatenate([piece, zero], axis=1))
        rows.append(jnp.concatenate([zero, piece], axis=1))
    return jnp.concatenate(rows, axis=0).astype(BF)


def second_tables():
    cosine, sine = lateral_angles()
    out = np.zeros((8, 8, 4, 4, 2, 4, M))
    for block in range(8):
        rows = slice(block * M, (block + 1) * M)
        for x in range(4):
            out[block, :, :, x, 0, x] = cosine[:, rows].reshape(8, 4, M)
            out[block, :, :, x, 1, x] = sine[:, rows].reshape(8, 4, M)
    out = out.reshape(8, 128, 256)
    return bf16(out), bf16(out.transpose(0, 2, 1))


def first_table():
    cosine, sine = lateral_angles()
    cos_x = cosine.T.reshape(M, 8, M).transpose(1, 0, 2)
    sin_x = sine.T.reshape(M, 8, M).transpose(1, 0, 2)
    out = np.zeros((8, M, 2, 2, 4, M))
    for j in range(4):
        out[:, :, 0, 0, j] = cos_x
        out[:, :, 0, 1, j] = -sin_x
        out[:, :, 1, 0, j] = sin_x
        out[:, :, 1, 1, j] = cos_x
    return bf16(out.reshape(512, 256))


def line_table():
    out = np.zeros((M, 2, 2, 2, 2, M))
    for k in range(M):
        for part in range(2):
            for x in range(2):
                out[k, part, x, part, x, k] = 1.0
    return bf16(out.reshape(64, 256))


def permutation(rows, lanes, sizes):
    total = int(np.prod([sizes[d] for d in rows]))
    position = np.arange(total).reshape([sizes[d] for d in rows])
    order = position.transpose([rows.index(d) for d in lanes]).reshape(-1)
    out = np.zeros((total, total))
    out[order, np.arange(total)] = 1.0
    return bf16(out)


def dot(a, b):
    return jnp.dot(a, b, preferred_element_type=F32)


def dot_nt(a, b):
    return lax.dot_general(a, b, (((1,), (1,)), ((), ())), preferred_element_type=F32)


def dot_tn(a, b):
    return lax.dot_general(a, b, (((0,), (0,)), ((), ())), preferred_element_type=F32)


def params(limit=40):
    return pltpu.CompilerParams(vmem_limit_bytes=limit * MIB)


def cost(flops, bytes_accessed, transcendentals=0):
    return pl.CostEstimate(
        flops=flops, bytes_accessed=bytes_accessed, transcendentals=transcendentals
    )


def whole(shape):
    return pl.BlockSpec(shape, lambda t, n: (0,) * len(shape))


def own(shape):
    return pl.BlockSpec((None,) + shape, lambda t, n: (n[0],) + (0,) * len(shape))


def second_forward(planes_ref, table, out_ref, first, count):
    for c in range(0, count, 2):
        one = planes_ref[first + c]
        two = planes_ref[first + c + 1]
        stacked = jnp.concatenate(
            [
                jnp.concatenate([one[:, :128], two[:, :128]], axis=1),
                jnp.concatenate([one[:, 128:], two[:, 128:]], axis=1),
            ],
            axis=0,
        )
        got = dot(table, stacked).astype(BF)
        for q in range(2):
            out_ref[:, (c + q) * 16 : (c + q + 1) * 16, :] = got[
                :, q * 128 : (q + 1) * 128
            ].reshape(8, 16, 128)


GRID = (C, 2, 4, M, N)
PARTS = C * 16
PAIR = PARTS + 16
STEP = 4
STEPS = C // STEP
FIELD_ROWS = STEP * 16
CARRY_ROWS = FIELD_ROWS + 32


VMEM = pl.BlockSpec(memory_space=pltpu.VMEM)
HBM = pl.BlockSpec(memory_space=pltpu.HBM)


def in_hbm(*arrays):
    return [pltpu.with_memory_space_constraint(jnp.asarray(a), pltpu.HBM) for a in arrays]


def analyse_kernel(
    block_ref,
    field_ref,
    weight_ref,
    depth_ref,
    table_ref,
    perm_ref,
    out_ref,
    planes_ref,
    rows_ref,
    depth_scratch,
):
    del block_ref

    @pl.when(pl.program_id(0) == 0)
    def _():
        rows_ref[...] = jnp.zeros((4, 256, M), F32)
        depth_scratch[...] = spread_depth(depth_ref[...])

    rows = jnp.concatenate([field_ref[:, x].reshape(STEP * 128, N) for x in range(2)], axis=1)
    planes_ref[...] = dot(rows, depth_scratch[...]).astype(BF).reshape(STEP, 128, N)
    second_forward(planes_ref, table_ref[...].astype(BF), out_ref, 0, STEP)
    got = jnp.zeros((128, 256), F32)
    for i in range(4):
        for q in range(8):
            rows_ref[i, q * CP : q * CP + C, :] = weight_ref[
                pl.ds(q * 4 * C + i, C, stride=4), :
            ]
        got = got + dot_nt(perm_ref[i].astype(BF), rows_ref[i].astype(BF))
    got = got.astype(BF)
    for b in range(2):
        out_ref[:, FIELD_ROWS + b * 16 : FIELD_ROWS + (b + 1) * 16, :] = got[
            :, b * 128 : (b + 1) * 128
        ].reshape(8, 16, 128)


def analyse(block, *operands):
    return pl.pallas_call(
        analyse_kernel,
        grid_spec=pltpu.PrefetchScalarGridSpec(
            num_scalar_prefetch=1,
            grid=(STEPS,),
            in_specs=[
                pl.BlockSpec((STEP, 2, 4, M, N), lambda t, n: (t, 0, 0, 0, 0)),
                pl.BlockSpec((32 * C, M), lambda t, n: (t, 0)),
                whole((N, 256)),
                own((128, 256)),
                whole((4, 128, M)),
            ],
            out_specs=pl.BlockSpec((8, CARRY_ROWS, 128), lambda t, n: (0, t, 0)),
            scratch_shapes=[
                pltpu.VMEM((STEP, 128, 256), BF),
                pltpu.VMEM((4, 256, M), F32),
                pltpu.VMEM((2 * N, 256), BF),
            ],
        ),
        out_shape=jax.ShapeDtypeStruct((8, STEPS * CARRY_ROWS, 128), BF),
        compiler_params=params(),
        cost_estimate=cost(2 * 20 * 256 * 256 * 256, 3 * MIB),
        name="analyse",
    )(block, *in_hbm(*operands))


def gather_kernel(stride, in_ref, perm_ref, out_ref, sum_ref, rows_ref):
    for t in range(STEPS):
        rows = slice(t * stride, t * stride + FIELD_ROWS)
        total = in_ref[0, rows].astype(F32)
        for source in range(1, 8):
            total = total + in_ref[source, rows].astype(F32)
        sum_ref[t * FIELD_ROWS : (t + 1) * FIELD_ROWS] = total
    rows_ref[...] = jnp.zeros((640, 256), BF)
    for x in range(4):
        rows = sum_ref[pl.ds(x, 80, stride=4), :].astype(BF)
        rows_ref[x * 80 : (x + 1) * 80, :128] = rows
        rows_ref[320 + x * 80 : 320 + (x + 1) * 80, 128:] = rows
    got = dot_nt(perm_ref[...].astype(BF), rows_ref[...])
    out_ref[...] = got.astype(BF).reshape(32, 2, 640)


def gather(parts, perm, stride):
    return pl.pallas_call(
        functools.partial(gather_kernel, stride),
        out_shape=jax.ShapeDtypeStruct((32, 2, 640), BF),
        scratch_shapes=[pltpu.VMEM((PARTS, 128), F32), pltpu.VMEM((640, 256), BF)],
        compiler_params=params(),
        cost_estimate=cost(2 * 128 * 128 * 512, MIB),
        name="gather",
    )(parts, perm)


def scatter_kernel(*refs):
    if len(refs) == 5:
        in_ref, perm_ref, pair_ref, out_ref, rows_ref = refs
        out_ref[:, PARTS:, :] = pair_ref[...]
    else:
        in_ref, perm_ref, out_ref, rows_ref = refs
    got = dot_tn(in_ref[...].reshape(64, 640), perm_ref[...].astype(BF))
    for x in range(4):
        rows_ref[pl.ds(x, 80, stride=4), :] = (
            got[x * 80 : (x + 1) * 80, :128] + got[320 + x * 80 : 320 + (x + 1) * 80, 128:]
        )
    value = rows_ref[...].astype(BF)
    for target in range(8):
        out_ref[target, :PARTS] = value


def scatter(lines, perm, *pair):
    return pl.pallas_call(
        scatter_kernel,
        out_shape=jax.ShapeDtypeStruct((8, PAIR if pair else PARTS, 128), BF),
        scratch_shapes=[pltpu.VMEM((PARTS, 128), F32)],
        compiler_params=params(),
        cost_estimate=cost(2 * 128 * 128 * 512, MIB),
        name="scatter",
    )(lines, perm, *pair)


def lane_group(shape):
    return lax.broadcasted_iota(jnp.int32, shape, 1) // M % 4


def to_modes(lines_ref, first, rows_ref):
    lines = lines_ref[...].reshape(64, 640).astype(F32).T.astype(BF)
    got = jnp.zeros((80, 256), F32)
    for x in range(8):
        got = got + dot(lines[x * 80 : (x + 1) * 80], first[x * 64 : (x + 1) * 64])
    group = lane_group((CP, 128))
    both = []
    for part in range(2):
        rows_ref[part, 0:80] = got[:, part * 128 : (part + 1) * 128]
        rows_ref[part, 80:] = jnp.zeros((16, 128), F32)
        out = jnp.zeros((CP, 128), F32)
        for j in range(4):
            out = jnp.where(group == j, rows_ref[part, pl.ds(j, CP, stride=4), :], out)
        both.append(jnp.concatenate([out, jnp.zeros((M - CP, 128), F32)], axis=0))
    return both


def from_modes(real, imag, first, rows_ref, lines_ref, out_ref):
    group = lane_group((CP, 128))
    for j in range(4):
        rows_ref[0, pl.ds(j, CP, stride=4), :] = jnp.where(group == j, real, 0.0)
        rows_ref[1, pl.ds(j, CP, stride=4), :] = jnp.where(group == j, imag, 0.0)
    both = jnp.concatenate([rows_ref[0, 0:80], rows_ref[1, 0:80]], axis=1)
    got = dot_nt(first, both.astype(BF))
    for x in range(8):
        lines_ref[:, x * 80 : (x + 1) * 80] = got[x * 64 : (x + 1) * 64]
    out_ref[...] = lines_ref[...].astype(BF).reshape(32, 2, 640)


def weight_row(part, c):
    index = part * C + c
    return (index // 8) * 256 + (index % 8) * CP


def mix_kernel(lines_ref, weight_ref, first_ref, out_ref, spectrum_ref, rows_ref, turned_ref):
    first = first_ref[...].astype(BF)
    real, imag = to_modes(lines_ref, first, rows_ref)
    spectrum_ref[0] = real
    spectrum_ref[1] = imag
    mixed_real = jnp.zeros((CP, 128), F32)
    mixed_imag = jnp.zeros((CP, 128), F32)
    for c in range(C):
        w0 = weight_ref[weight_row(0, c) : weight_row(0, c) + CP, :]
        w1 = weight_ref[weight_row(1, c) : weight_row(1, c) + CP, :]
        s0 = real[c : c + 1]
        s1 = imag[c : c + 1]
        mixed_real = mixed_real + s0 * w0 - s1 * w1
        mixed_imag = mixed_imag + s0 * w1 + s1 * w0
    from_modes(mixed_real, mixed_imag, first, rows_ref, turned_ref, out_ref)


def mix_back_kernel(
    lines_ref,
    weight_ref,
    first_ref,
    spectrum_ref,
    perm_ref,
    out_ref,
    pair_ref,
    acc_ref,
    rows_ref,
    turned_ref,
):
    first = first_ref[...].astype(BF)
    real, imag = to_modes(lines_ref, first, rows_ref)
    both = jnp.concatenate([spectrum_ref[0], spectrum_ref[1], real, imag], axis=0)
    pair_ref[...] = dot_nt(perm_ref[...].astype(BF), both.astype(BF)).astype(BF).reshape(8, 16, 128)
    r0 = real[:CP]
    r1 = imag[:CP]
    acc_ref[...] = jnp.zeros((2, CP, 128), F32)
    for c in range(C):
        w0 = weight_ref[weight_row(0, c) : weight_row(0, c) + CP, :]
        w1 = weight_ref[weight_row(1, c) : weight_row(1, c) + CP, :]
        acc_ref[0, c : c + 1, :] = jnp.sum(r0 * w0 + r1 * w1, axis=0, keepdims=True)
        acc_ref[1, c : c + 1, :] = jnp.sum(r1 * w0 - r0 * w1, axis=0, keepdims=True)
    from_modes(acc_ref[0], acc_ref[1], first, rows_ref, turned_ref, out_ref)


def mix(*operands):
    return pl.pallas_call(
        mix_kernel,
        out_shape=[
            jax.ShapeDtypeStruct((32, 2, 640), BF),
            jax.ShapeDtypeStruct((2, M, 128), F32),
        ],
        scratch_shapes=[pltpu.VMEM((2, 4 * CP, 128), F32), pltpu.VMEM((64, 640), F32)],
        compiler_params=params(),
        cost_estimate=cost(4 * 512 * 128 * 256, 2 * MIB),
        name="mix",
    )(*operands)


def mix_back(*operands):
    return pl.pallas_call(
        mix_back_kernel,
        out_shape=[
            jax.ShapeDtypeStruct((32, 2, 640), BF),
            jax.ShapeDtypeStruct((8, 16, 128), BF),
        ],
        scratch_shapes=[
            pltpu.VMEM((2, CP, 128), F32),
            pltpu.VMEM((2, 4 * CP, 128), F32),
            pltpu.VMEM((64, 640), F32),
        ],
        compiler_params=params(),
        cost_estimate=cost(4 * 512 * 128 * 256, 2 * MIB),
        name="mix_back",
    )(*operands)


def widen(local, transposed):
    row = lax.broadcasted_iota(jnp.int32, (C * 16, C), 0)
    channel = lax.broadcasted_iota(jnp.int32, (C * 16, C), 1)
    spread = jnp.where(row // 16 == channel, 1.0, 0.0).astype(BF)
    multiply = dot_nt if transposed else dot
    rows = multiply(spread, local).astype(BF)
    row = lax.broadcasted_iota(jnp.int32, (C * 16, C * 16), 0)
    lane = lax.broadcasted_iota(jnp.int32, (C * 16, C * 16), 1)
    return jnp.where(row % 16 == lane % 16, dot_nt(rows, spread), 0.0).astype(BF)


def weight_in_kernel(
    block_ref,
    in_ref,
    perm_ref,
    synth_ref,
    depth_ref,
    table_ref,
    inverse_ref,
    back_ref,
    local_ref,
    out_ref,
    synth_out,
    depth_out,
    table_out,
    inverse_out,
    back_out,
    wide_out,
    wide_back_out,
):
    del block_ref

    @pl.when(pl.program_id(0) == 0)
    def _():
        synth_out[...] = spread_synth(synth_ref[...])
        depth_out[...] = spread_depth(depth_ref[...])
        table_out[...] = table_ref[...].astype(BF)
        inverse_out[...] = inverse_ref[...].astype(BF)
        back_out[...] = spread_synth(back_ref[...])
        wide_out[...] = widen(local_ref[...], False)
        wide_back_out[...] = widen(local_ref[...], True)

    perm = perm_ref[...].astype(BF)
    for b in range(2):
        start = FIELD_ROWS + b * 16
        rows = in_ref[:, start : start + 16, :].reshape(128, 128)
        out_ref[b * 128 : (b + 1) * 128] = dot_tn(rows, perm)


def weight_in(block, parts, perm, *tables):
    shapes = [(128, 512), (2 * N, 256), (128, 256), (256, 128), (128, 512)]
    shapes += [(C * 16, C * 16)] * 2
    return pl.pallas_call(
        weight_in_kernel,
        grid_spec=pltpu.PrefetchScalarGridSpec(
            num_scalar_prefetch=1,
            grid=(STEPS,),
            in_specs=[
                pl.BlockSpec((8, CARRY_ROWS, 128), lambda t, n: (0, t, 0)),
                whole((128, 128)),
                whole((2 * M, N)),
                whole((N, 256)),
                own((128, 256)),
                own((256, 128)),
                whole((2 * M, N)),
                whole((C, C)),
            ],
            out_specs=[pl.BlockSpec((256, 128), lambda t, n: (t, 0))] + [whole(s) for s in shapes],
        ),
        out_shape=[jax.ShapeDtypeStruct((STEPS * 256, 128), F32)]
        + [jax.ShapeDtypeStruct(s, BF) for s in shapes],
        compiler_params=params(16),
        cost_estimate=cost(2 * 128 * 128 * 1280, 3 * MIB),
        name="weight_in",
    )(block, parts, *in_hbm(perm, *tables))


def second_inverse(in_ref, table, planes_ref):
    lane = lax.broadcasted_iota(jnp.int32, (128, 256), 1) % 128
    for c in range(0, C, 2):
        both = jnp.concatenate(
            [in_ref[:, (c + q) * 16 : (c + q + 1) * 16, :].reshape(128, 128) for q in range(2)],
            axis=1,
        )
        got = dot(table, both)
        for q in range(2):
            cos_part = got[:128, q * 128 : (q + 1) * 128]
            sin_part = got[128:, q * 128 : (q + 1) * 128]
            turned = pltpu.roll(sin_part, 64, 1)
            value = jnp.where(lane[:, :128] < 64, cos_part - turned, cos_part + turned)
            planes_ref[c + q] = value.astype(BF)


def piece(ref, t):
    return ref.at[:, :, t // 2, pl.ds(pl.multiple_of((t % 2) * 16, 16), 16), :]


def moving(source, target, t, sem):
    return pltpu.make_async_copy(piece(source, t), piece(target, t), sem.at[t])


def local_kernel(
    parts_ref,
    field_hbm,
    cotangent_hbm,
    synth_ref,
    depth_ref,
    table_ref,
    inverse_ref,
    wide_ref,
    wide_back_ref,
    bias_ref,
    activated_hbm,
    mixed_ref,
    out_ref,
    planes_ref,
    turned_ref,
    field_ref,
    cotangent_ref,
    activated_ref,
    field_sem,
    cotangent_sem,
    activated_sem,
):
    for t in range(8):
        moving(field_hbm, field_ref, t, field_sem).start()
        moving(cotangent_hbm, cotangent_ref, t, cotangent_sem).start()
    second_inverse(parts_ref, inverse_ref[...], planes_ref)
    scale = 0.7978845608028654
    cubic = scale * 0.044715

    def step(t, carry):
        moving(field_hbm, field_ref, t, field_sem).wait()
        moving(cotangent_hbm, cotangent_ref, t, cotangent_sem).wait()
        y = pl.ds(pl.multiple_of((t % 2) * 16, 16), 16)
        rows = pl.ds(pl.multiple_of(t * 16, 16), 16)
        planes = planes_ref[:, rows, :].reshape(C * 16, 128)
        left = jnp.concatenate([planes, wide_ref[...]], axis=1)
        slopes = []
        for x in range(2):
            field = field_ref[:, x, t // 2, y, :].reshape(C * 16, N)
            right = jnp.concatenate([synth_ref[:, x * N : (x + 1) * N], field], axis=0)
            values = dot(left, right)
            pieces = []
            for c in range(C):
                value = values[c * 16 : (c + 1) * 16] + bias_ref[c]
                square = value * value
                half = 0.5 + 0.5 * jnp.tanh(value * (scale + cubic * square))
                activated = value * half
                activated_ref[c, x, t // 2, y, :] = activated.astype(BF)
                d_inner = (2.0 * scale) + (6.0 * cubic) * square
                d_gelu = half + (activated * (1.0 - half)) * d_inner
                pieces.append((cotangent_ref[c, x, t // 2, y, :].astype(F32) * d_gelu).astype(BF))
            slope = jnp.concatenate(pieces, axis=0)
            slopes.append(slope)
            mixed = dot(wide_back_ref[...], slope).astype(BF)
            mixed_ref[:, x, t // 2, y, :] = mixed.reshape(C, 16, N)
        moving(activated_ref, activated_hbm, t, activated_sem).start()
        response = dot(jnp.concatenate(slopes, axis=1), depth_ref[...])
        turned_ref[:, rows, :] = response.astype(BF).reshape(C, 16, 256)
        return carry

    lax.fori_loop(0, 8, step, 0)
    second_forward(turned_ref, table_ref[...], out_ref, 0, C)
    for t in range(8):
        moving(activated_ref, activated_hbm, t, activated_sem).wait()


def local(parts, field, cotangent, *operands):
    return pl.pallas_call(
        local_kernel,
        in_specs=[VMEM, HBM, HBM] + [VMEM] * 6 + [pl.BlockSpec(memory_space=pltpu.SMEM)],
        out_specs=[HBM, VMEM, VMEM],
        out_shape=[
            pltpu.HBM(GRID, BF),
            jax.ShapeDtypeStruct(GRID, BF),
            jax.ShapeDtypeStruct((8, PARTS, 128), BF),
        ],
        scratch_shapes=[pltpu.VMEM((C, 128, 128), BF), pltpu.VMEM((C, 128, 256), BF)]
        + [pltpu.VMEM(GRID, BF)] * 3
        + [pltpu.SemaphoreType.DMA((8,))] * 3,
        compiler_params=params(24),
        cost_estimate=cost(3 * 10**9, 12 * MIB, 1310720),
        name="local",
    )(parts, *in_hbm(field, cotangent), *operands)


def local_back_kernel(
    parts_ref,
    mixed_ref,
    synth_ref,
    inverse_ref,
    perm_ref,
    out_hbm,
    grad_hbm,
    planes_ref,
    modes_ref,
    out_ref,
    grad_ref,
    out_sem,
    grad_sem,
):
    pair = parts_ref[:, PARTS:, :].reshape(128, 128)
    for i in range(4):
        modes_ref[pl.ds(i, 128, stride=4), :] = dot_tn(pair, perm_ref[i].astype(BF))
    r0 = modes_ref[8 * M : 8 * M + 4 * C, :]
    r1 = modes_ref[12 * M : 12 * M + 4 * C, :]

    def outer(t):
        return pltpu.make_async_copy(
            grad_ref.at[:, pl.ds(t * 5, 5)], grad_hbm.at[:, pl.ds(t * 5, 5)], grad_sem.at[t]
        )

    for c in range(C):
        s0 = jnp.concatenate([modes_ref[c * 4 : c * 4 + 4, :]] * C, axis=0)
        s1 = jnp.concatenate([modes_ref[4 * M + c * 4 : 4 * M + c * 4 + 4, :]] * C, axis=0)
        grad_ref[0, c] = s0 * r0 + s1 * r1
        grad_ref[1, c] = s0 * r1 - s1 * r0
        if c % 5 == 4:
            outer(c // 5).start()

    second_inverse(parts_ref, inverse_ref[...], planes_ref)

    def step(t, carry):
        y = pl.ds(pl.multiple_of((t % 2) * 16, 16), 16)
        rows = pl.ds(pl.multiple_of(t * 16, 16), 16)
        planes = planes_ref[:, rows, :].reshape(C * 16, 128)
        spatial = dot(planes, synth_ref[...])
        for x in range(2):
            for c in range(C):
                value = spatial[c * 16 : (c + 1) * 16, x * N : (x + 1) * N]
                value = value + mixed_ref[c, x, t // 2, y, :].astype(F32)
                out_ref[c, x, t // 2, y, :] = value.astype(BF)
        moving(out_ref, out_hbm, t, out_sem).start()
        return carry

    lax.fori_loop(0, 8, step, 0, unroll=4)
    for t in range(8):
        moving(out_ref, out_hbm, t, out_sem).wait()
    for t in range(4):
        outer(t).wait()


def local_back(parts, mixed, *tables):
    grad = (2, C, 4 * C, M)
    return pl.pallas_call(
        local_back_kernel,
        in_specs=[VMEM] * (2 + len(tables)),
        out_specs=[HBM, HBM],
        out_shape=[pltpu.HBM(GRID, BF), pltpu.HBM(grad, F32)],
        scratch_shapes=[
            pltpu.VMEM((C, 128, 128), BF),
            pltpu.VMEM((512, M), F32),
            pltpu.VMEM(GRID, BF),
            pltpu.VMEM(grad, F32),
            pltpu.SemaphoreType.DMA((8,)),
            pltpu.SemaphoreType.DMA((4,)),
        ],
        compiler_params=params(24),
        cost_estimate=cost(2 * 10**9, 6 * MIB),
        name="local_back",
    )(parts, mixed, *tables)


def exchange(value, axis):
    return lax.all_to_all(value, axis, split_axis=0, concat_axis=0, tiled=True)


def shards(field, cotangent, spectral_weight, local_weight, local_bias):
    forward, inverse = depth_tables()
    forward_b, inverse_b = analysis_depth(forward), analysis_depth(inverse.T)
    synth_f, synth_b = bf16(inverse), bf16(forward.T)
    second, second_back = second_tables()
    first = first_table()
    block = lax.axis_index("narrow").astype(jnp.int32).reshape(1)

    sizes = {"J": 8, "j": 4, "i": 4}
    perm_line = line_table()
    perm_weight = permutation("Jji", "iJj", sizes)
    perm_modes = permutation("Jji", "jJi", sizes)
    perm_grad = np.stack([perm_weight[:, i * M : (i + 1) * M] for i in range(4)])

    shape = field.shape
    grid_field = field.reshape(GRID)
    grid_cotangent = cotangent.reshape(GRID)

    weight = jnp.transpose(spectral_weight, (0, 1, 2, 3, 5, 4)).reshape(8 * C * C, M)
    parts = exchange(analyse(block, grid_field, weight, forward_b, second, perm_grad), "narrow")
    weight, synth, depth, table, table_back, back, wide, wide_back = weight_in(
        block, parts, perm_modes, synth_f, inverse_b, second, second_back, synth_b, local_weight
    )
    lines = exchange(gather(parts, perm_line, CARRY_ROWS), "wide")
    lines, spectrum = mix(lines, weight, first)
    lines = exchange(lines, "wide")
    parts = exchange(scatter(lines, perm_line), "narrow")
    activated, mixed, parts = local(
        parts,
        grid_field,
        grid_cotangent,
        synth,
        depth,
        table,
        table_back,
        wide,
        wide_back,
        local_bias,
    )
    parts = exchange(parts, "narrow")
    lines = exchange(gather(parts, perm_line, FIELD_ROWS), "wide")
    lines, pair = mix_back(lines, weight, first, spectrum, perm_modes)
    lines = exchange(lines, "wide")
    parts = exchange(scatter(lines, perm_line, pair), "narrow")
    field_grad, weight_grad = local_back(parts, mixed, back, table_back, perm_grad)
    return (
        activated.reshape(shape),
        field_grad.reshape(shape),
        weight_grad.reshape(spectral_weight.shape),
    )


def solution(mesh):
    return jax.shard_map(
        shards,
        mesh=mesh,
        in_specs=(
            P(None, "wide", "narrow", None),
            P(None, "wide", "narrow", None),
            P(None, None, None, "narrow", None, "wide"),
            P(),
            P(),
        ),
        out_specs=(
            P(None, "wide", "narrow", None),
            P(None, "wide", "narrow", None),
            P(None, None, None, "narrow", None, "wide"),
        ),
        check_vma=False,
    )
```

```python
import functools
import math

import jax
import jax.numpy as jnp
import ml_dtypes
import numpy as np
from jax import lax
from jax.experimental import pallas as pl
from jax.experimental.pallas import tpu as pltpu
from jax.sharding import PartitionSpec as P

N = 256
M = 32
C = 20
CP = 24
BF = jnp.bfloat16
F32 = jnp.float32
MIB = 1024 * 1024


def depth_tables():
    index = np.arange(N)
    freq = np.arange(M)
    angle = (2.0 * math.pi / N) * ((freq[:, None] * index[None, :]) % N)
    scale = 1.0 / math.sqrt(N)
    weights = np.where(freq == 0, 1.0, 2.0)[:, None]
    forward = (np.concatenate([np.cos(angle), -np.sin(angle)]) * scale).T
    inverse = np.concatenate([weights * np.cos(angle), -weights * np.sin(angle)]) * scale
    return forward, inverse


def lateral_angles():
    index = np.arange(N)
    base = np.arange(M)
    freq = np.where(base < M // 2, base, N - M + base)
    angle = (2.0 * math.pi / N) * ((freq[:, None] * index[None, :]) % N)
    scale = 1.0 / math.sqrt(N)
    return np.cos(angle) * scale, np.sin(angle) * scale


def bf16(array):
    return np.asarray(array, np.float32).astype(ml_dtypes.bfloat16).astype(np.float32)


def analysis_depth(table):
    out = np.zeros((N, 2, 2, 2, M))
    real, imag = table[:, :M], table[:, M:]
    out[:, 0, 0, 0] = real
    out[:, 0, 1, 0] = imag
    out[:, 1, 0, 0] = imag
    out[:, 1, 1, 0] = -real
    return bf16(out.reshape(N, 256))


def spread_depth(table):
    return jnp.concatenate([table, pltpu.roll(table, M, 1)], axis=0).astype(BF)


def spread_synth(table):
    zero = jnp.zeros((M, N), F32)
    rows = []
    for part in range(2):
        piece = table[part * M : (part + 1) * M]
        rows.append(jnp.concatenate([piece, zero], axis=1))
        rows.append(jnp.concatenate([zero, piece], axis=1))
    return jnp.concatenate(rows, axis=0).astype(BF)


def second_tables():
    cosine, sine = lateral_angles()
    out = np.zeros((8, 8, 4, 4, 2, 4, M))
    for block in range(8):
        rows = slice(block * M, (block + 1) * M)
        for x in range(4):
            out[block, :, :, x, 0, x] = cosine[:, rows].reshape(8, 4, M)
            out[block, :, :, x, 1, x] = sine[:, rows].reshape(8, 4, M)
    out = out.reshape(8, 128, 256)
    return bf16(out), bf16(out.transpose(0, 2, 1))


def first_table():
    cosine, sine = lateral_angles()
    cos_x = cosine.T.reshape(M, 8, M).transpose(1, 0, 2)
    sin_x = sine.T.reshape(M, 8, M).transpose(1, 0, 2)
    out = np.zeros((8, M, 2, 2, 4, M))
    for j in range(4):
        out[:, :, 0, 0, j] = cos_x
        out[:, :, 0, 1, j] = -sin_x
        out[:, :, 1, 0, j] = sin_x
        out[:, :, 1, 1, j] = cos_x
    return bf16(out.reshape(512, 256))


def line_table():
    out = np.zeros((M, 2, 2, 2, 2, M))
    for k in range(M):
        for part in range(2):
            for x in range(2):
                out[k, part, x, part, x, k] = 1.0
    return bf16(out.reshape(64, 256))


def permutation(rows, lanes, sizes):
    total = int(np.prod([sizes[d] for d in rows]))
    position = np.arange(total).reshape([sizes[d] for d in rows])
    order = position.transpose([rows.index(d) for d in lanes]).reshape(-1)
    out = np.zeros((total, total))
    out[order, np.arange(total)] = 1.0
    return bf16(out)


def dot(a, b):
    return jnp.dot(a, b, preferred_element_type=F32)


def dot_nt(a, b):
    return lax.dot_general(a, b, (((1,), (1,)), ((), ())), preferred_element_type=F32)


def dot_tn(a, b):
    return lax.dot_general(a, b, (((0,), (0,)), ((), ())), preferred_element_type=F32)


def params(limit=40):
    return pltpu.CompilerParams(vmem_limit_bytes=limit * MIB)


def cost(flops, bytes_accessed, transcendentals=0):
    return pl.CostEstimate(
        flops=flops, bytes_accessed=bytes_accessed, transcendentals=transcendentals
    )


def whole(shape):
    return pl.BlockSpec(shape, lambda t, n: (0,) * len(shape))


def own(shape):
    return pl.BlockSpec((None,) + shape, lambda t, n: (n[0],) + (0,) * len(shape))


def second_forward(planes_ref, table, out_ref, first, count):
    for c in range(0, count, 2):
        one = planes_ref[first + c]
        two = planes_ref[first + c + 1]
        stacked = jnp.concatenate(
            [
                jnp.concatenate([one[:, :128], two[:, :128]], axis=1),
                jnp.concatenate([one[:, 128:], two[:, 128:]], axis=1),
            ],
            axis=0,
        )
        got = dot(table, stacked).astype(BF)
        for q in range(2):
            out_ref[:, (c + q) * 16 : (c + q + 1) * 16, :] = got[
                :, q * 128 : (q + 1) * 128
            ].reshape(8, 16, 128)


GRID = (C, 2, 4, M, N)
PARTS = C * 16
PAIR = PARTS + 16
STEP = 4
STEPS = C // STEP
FIELD_ROWS = STEP * 16
CARRY_ROWS = FIELD_ROWS + 32


VMEM = pl.BlockSpec(memory_space=pltpu.VMEM)
HBM = pl.BlockSpec(memory_space=pltpu.HBM)


def in_hbm(*arrays):
    return [pltpu.with_memory_space_constraint(jnp.asarray(a), pltpu.HBM) for a in arrays]


def analyse_kernel(
    block_ref,
    field_ref,
    weight_ref,
    depth_ref,
    table_ref,
    perm_ref,
    out_ref,
    planes_ref,
    rows_ref,
    depth_scratch,
    table_scratch,
    perm_scratch,
):
    del block_ref

    @pl.when(pl.program_id(0) == 0)
    def _():
        rows_ref[...] = jnp.zeros((4, 256, M), F32)
        depth_scratch[...] = spread_depth(depth_ref[...])
        table_scratch[...] = table_ref[...].astype(BF)
        perm_scratch[...] = perm_ref[...].astype(BF)

    rows = jnp.concatenate([field_ref[:, x].reshape(STEP * 128, N) for x in range(2)], axis=1)
    planes_ref[...] = dot(rows, depth_scratch[...]).astype(BF).reshape(STEP, 128, N)
    second_forward(planes_ref, table_scratch[...], out_ref, 0, STEP)
    got = jnp.zeros((128, 256), F32)
    for i in range(4):
        for q in range(8):
            rows_ref[i, q * CP : q * CP + C, :] = weight_ref[
                pl.ds(q * 4 * C + i, C, stride=4), :
            ]
        got = got + dot_nt(perm_scratch[i], rows_ref[i].astype(BF))
    got = got.astype(BF)
    for b in range(2):
        out_ref[:, FIELD_ROWS + b * 16 : FIELD_ROWS + (b + 1) * 16, :] = got[
            :, b * 128 : (b + 1) * 128
        ].reshape(8, 16, 128)


def analyse(block, *operands):
    return pl.pallas_call(
        analyse_kernel,
        grid_spec=pltpu.PrefetchScalarGridSpec(
            num_scalar_prefetch=1,
            grid=(STEPS,),
            in_specs=[
                pl.BlockSpec((STEP, 2, 4, M, N), lambda t, n: (t, 0, 0, 0, 0)),
                pl.BlockSpec((32 * C, M), lambda t, n: (t, 0)),
                whole((N, 256)),
                own((128, 256)),
                whole((4, 128, M)),
            ],
            out_specs=pl.BlockSpec((8, CARRY_ROWS, 128), lambda t, n: (0, t, 0)),
            scratch_shapes=[
                pltpu.VMEM((STEP, 128, 256), BF),
                pltpu.VMEM((4, 256, M), F32),
                pltpu.VMEM((2 * N, 256), BF),
                pltpu.VMEM((128, 256), BF),
                pltpu.VMEM((4, 128, M), BF),
            ],
        ),
        out_shape=jax.ShapeDtypeStruct((8, STEPS * CARRY_ROWS, 128), BF),
        compiler_params=params(),
        cost_estimate=cost(2 * 20 * 256 * 256 * 256, 3 * MIB),
        name="analyse",
    )(block, *in_hbm(*operands))


def gather_kernel(stride, in_ref, perm_ref, out_ref, sum_ref, rows_ref):
    for t in range(STEPS):
        rows = slice(t * stride, t * stride + FIELD_ROWS)
        total = in_ref[0, rows].astype(F32)
        for source in range(1, 8):
            total = total + in_ref[source, rows].astype(F32)
        sum_ref[t * FIELD_ROWS : (t + 1) * FIELD_ROWS] = total
    rows_ref[...] = jnp.zeros((640, 256), BF)
    for x in range(4):
        rows = sum_ref[pl.ds(x, 80, stride=4), :].astype(BF)
        rows_ref[x * 80 : (x + 1) * 80, :128] = rows
        rows_ref[320 + x * 80 : 320 + (x + 1) * 80, 128:] = rows
    got = dot_nt(perm_ref[...].astype(BF), rows_ref[...])
    out_ref[...] = got.astype(BF).reshape(32, 2, 640)


def gather(parts, perm, stride):
    return pl.pallas_call(
        functools.partial(gather_kernel, stride),
        out_shape=jax.ShapeDtypeStruct((32, 2, 640), BF),
        scratch_shapes=[pltpu.VMEM((PARTS, 128), F32), pltpu.VMEM((640, 256), BF)],
        compiler_params=params(),
        cost_estimate=cost(2 * 128 * 128 * 512, MIB),
        name="gather",
    )(parts, perm)


def scatter_kernel(*refs):
    if len(refs) == 5:
        in_ref, perm_ref, pair_ref, out_ref, rows_ref = refs
        out_ref[:, PARTS:, :] = pair_ref[...]
    else:
        in_ref, perm_ref, out_ref, rows_ref = refs
    got = dot_tn(in_ref[...].reshape(64, 640), perm_ref[...].astype(BF))
    for x in range(4):
        rows_ref[pl.ds(x, 80, stride=4), :] = (
            got[x * 80 : (x + 1) * 80, :128] + got[320 + x * 80 : 320 + (x + 1) * 80, 128:]
        )
    value = rows_ref[...].astype(BF)
    for target in range(8):
        out_ref[target, :PARTS] = value


def scatter(lines, perm, *pair):
    return pl.pallas_call(
        scatter_kernel,
        out_shape=jax.ShapeDtypeStruct((8, PAIR if pair else PARTS, 128), BF),
        scratch_shapes=[pltpu.VMEM((PARTS, 128), F32)],
        compiler_params=params(),
        cost_estimate=cost(2 * 128 * 128 * 512, MIB),
        name="scatter",
    )(lines, perm, *pair)


def lane_group(shape):
    return lax.broadcasted_iota(jnp.int32, shape, 1) // M % 4


def to_modes(lines_ref, first, rows_ref):
    lines = lines_ref[...].reshape(64, 640).astype(F32).T.astype(BF)
    got = jnp.zeros((80, 256), F32)
    for x in range(8):
        got = got + dot(lines[x * 80 : (x + 1) * 80], first[x * 64 : (x + 1) * 64])
    group = lane_group((CP, 128))
    both = []
    for part in range(2):
        rows_ref[part, 0:80] = got[:, part * 128 : (part + 1) * 128]
        rows_ref[part, 80:] = jnp.zeros((16, 128), F32)
        out = jnp.zeros((CP, 128), F32)
        for j in range(4):
            out = jnp.where(group == j, rows_ref[part, pl.ds(j, CP, stride=4), :], out)
        both.append(jnp.concatenate([out, jnp.zeros((M - CP, 128), F32)], axis=0))
    return both


def from_modes(real, imag, first, rows_ref, lines_ref, out_ref):
    group = lane_group((CP, 128))
    for j in range(4):
        rows_ref[0, pl.ds(j, CP, stride=4), :] = jnp.where(group == j, real, 0.0)
        rows_ref[1, pl.ds(j, CP, stride=4), :] = jnp.where(group == j, imag, 0.0)
    both = jnp.concatenate([rows_ref[0, 0:80], rows_ref[1, 0:80]], axis=1)
    got = dot_nt(first, both.astype(BF))
    for x in range(8):
        lines_ref[:, x * 80 : (x + 1) * 80] = got[x * 64 : (x + 1) * 64]
    out_ref[...] = lines_ref[...].astype(BF).reshape(32, 2, 640)


def weight_row(part, c):
    index = part * C + c
    return (index // 8) * 256 + (index % 8) * CP


def mix_kernel(lines_ref, weight_ref, first_ref, out_ref, spectrum_ref, rows_ref, turned_ref):
    first = first_ref[...].astype(BF)
    real, imag = to_modes(lines_ref, first, rows_ref)
    spectrum_ref[0] = real
    spectrum_ref[1] = imag
    mixed_real = jnp.zeros((CP, 128), F32)
    mixed_imag = jnp.zeros((CP, 128), F32)
    for c in range(C):
        w0 = weight_ref[weight_row(0, c) : weight_row(0, c) + CP, :]
        w1 = weight_ref[weight_row(1, c) : weight_row(1, c) + CP, :]
        s0 = real[c : c + 1]
        s1 = imag[c : c + 1]
        mixed_real = mixed_real + s0 * w0 - s1 * w1
        mixed_imag = mixed_imag + s0 * w1 + s1 * w0
    from_modes(mixed_real, mixed_imag, first, rows_ref, turned_ref, out_ref)


def mix_back_kernel(
    lines_ref,
    weight_ref,
    first_ref,
    spectrum_ref,
    perm_ref,
    out_ref,
    pair_ref,
    acc_ref,
    rows_ref,
    turned_ref,
):
    first = first_ref[...].astype(BF)
    real, imag = to_modes(lines_ref, first, rows_ref)
    both = jnp.concatenate([spectrum_ref[0], spectrum_ref[1], real, imag], axis=0)
    pair_ref[...] = dot_nt(perm_ref[...].astype(BF), both.astype(BF)).astype(BF).reshape(8, 16, 128)
    r0 = real[:CP]
    r1 = imag[:CP]
    acc_ref[...] = jnp.zeros((2, CP, 128), F32)
    for c in range(C):
        w0 = weight_ref[weight_row(0, c) : weight_row(0, c) + CP, :]
        w1 = weight_ref[weight_row(1, c) : weight_row(1, c) + CP, :]
        acc_ref[0, c : c + 1, :] = jnp.sum(r0 * w0 + r1 * w1, axis=0, keepdims=True)
        acc_ref[1, c : c + 1, :] = jnp.sum(r1 * w0 - r0 * w1, axis=0, keepdims=True)
    from_modes(acc_ref[0], acc_ref[1], first, rows_ref, turned_ref, out_ref)


def mix(*operands):
    return pl.pallas_call(
        mix_kernel,
        out_shape=[
            jax.ShapeDtypeStruct((32, 2, 640), BF),
            jax.ShapeDtypeStruct((2, M, 128), F32),
        ],
        scratch_shapes=[pltpu.VMEM((2, 4 * CP, 128), F32), pltpu.VMEM((64, 640), F32)],
        compiler_params=params(),
        cost_estimate=cost(4 * 512 * 128 * 256, 2 * MIB),
        name="mix",
    )(*operands)


def mix_back(*operands):
    return pl.pallas_call(
        mix_back_kernel,
        out_shape=[
            jax.ShapeDtypeStruct((32, 2, 640), BF),
            jax.ShapeDtypeStruct((8, 16, 128), BF),
        ],
        scratch_shapes=[
            pltpu.VMEM((2, CP, 128), F32),
            pltpu.VMEM((2, 4 * CP, 128), F32),
            pltpu.VMEM((64, 640), F32),
        ],
        compiler_params=params(),
        cost_estimate=cost(4 * 512 * 128 * 256, 2 * MIB),
        name="mix_back",
    )(*operands)


def widen(local, transposed):
    row = lax.broadcasted_iota(jnp.int32, (C * 16, C), 0)
    channel = lax.broadcasted_iota(jnp.int32, (C * 16, C), 1)
    spread = jnp.where(row // 16 == channel, 1.0, 0.0).astype(BF)
    multiply = dot_nt if transposed else dot
    rows = multiply(spread, local).astype(BF)
    row = lax.broadcasted_iota(jnp.int32, (C * 16, C * 16), 0)
    lane = lax.broadcasted_iota(jnp.int32, (C * 16, C * 16), 1)
    return jnp.where(row % 16 == lane % 16, dot_nt(rows, spread), 0.0).astype(BF)


def weight_in_kernel(
    block_ref,
    in_ref,
    perm_ref,
    synth_ref,
    depth_ref,
    table_ref,
    inverse_ref,
    back_ref,
    local_ref,
    out_ref,
    synth_out,
    depth_out,
    table_out,
    inverse_out,
    back_out,
    wide_out,
    wide_back_out,
):
    del block_ref

    @pl.when(pl.program_id(0) == 0)
    def _():
        synth_out[...] = spread_synth(synth_ref[...])
        depth_out[...] = spread_depth(depth_ref[...])
        table_out[...] = table_ref[...].astype(BF)
        inverse_out[...] = inverse_ref[...].astype(BF)
        back_out[...] = spread_synth(back_ref[...])
        wide_out[...] = widen(local_ref[...], False)
        wide_back_out[...] = widen(local_ref[...], True)

    perm = perm_ref[...].astype(BF)
    for b in range(2):
        start = FIELD_ROWS + b * 16
        rows = in_ref[:, start : start + 16, :].reshape(128, 128)
        out_ref[b * 128 : (b + 1) * 128] = dot_tn(rows, perm)


def weight_in(block, parts, perm, *tables):
    shapes = [(128, 512), (2 * N, 256), (128, 256), (256, 128), (128, 512)]
    shapes += [(C * 16, C * 16)] * 2
    return pl.pallas_call(
        weight_in_kernel,
        grid_spec=pltpu.PrefetchScalarGridSpec(
            num_scalar_prefetch=1,
            grid=(STEPS,),
            in_specs=[
                pl.BlockSpec((8, CARRY_ROWS, 128), lambda t, n: (0, t, 0)),
                whole((128, 128)),
                whole((2 * M, N)),
                whole((N, 256)),
                own((128, 256)),
                own((256, 128)),
                whole((2 * M, N)),
                whole((C, C)),
            ],
            out_specs=[pl.BlockSpec((256, 128), lambda t, n: (t, 0))] + [whole(s) for s in shapes],
        ),
        out_shape=[jax.ShapeDtypeStruct((STEPS * 256, 128), F32)]
        + [jax.ShapeDtypeStruct(s, BF) for s in shapes],
        compiler_params=params(16),
        cost_estimate=cost(2 * 128 * 128 * 1280, 3 * MIB),
        name="weight_in",
    )(block, parts, *in_hbm(perm, *tables))


def second_inverse(in_ref, table, planes_ref):
    lane = lax.broadcasted_iota(jnp.int32, (128, 256), 1) % 128
    for c in range(0, C, 2):
        both = jnp.concatenate(
            [in_ref[:, (c + q) * 16 : (c + q + 1) * 16, :].reshape(128, 128) for q in range(2)],
            axis=1,
        )
        got = dot(table, both)
        for q in range(2):
            cos_part = got[:128, q * 128 : (q + 1) * 128]
            sin_part = got[128:, q * 128 : (q + 1) * 128]
            turned = pltpu.roll(sin_part, 64, 1)
            value = jnp.where(lane[:, :128] < 64, cos_part - turned, cos_part + turned)
            planes_ref[c + q] = value.astype(BF)


def piece(ref, t):
    return ref.at[:, :, t // 2, pl.ds(pl.multiple_of((t % 2) * 16, 16), 16), :]


def moving(source, target, t, sem):
    return pltpu.make_async_copy(piece(source, t), piece(target, t), sem.at[t])


def local_kernel(
    parts_ref,
    field_hbm,
    cotangent_hbm,
    synth_ref,
    depth_ref,
    table_ref,
    inverse_ref,
    wide_ref,
    wide_back_ref,
    bias_ref,
    activated_hbm,
    mixed_ref,
    out_ref,
    planes_ref,
    turned_ref,
    field_ref,
    cotangent_ref,
    activated_ref,
    field_sem,
    cotangent_sem,
    activated_sem,
):
    for t in range(8):
        moving(field_hbm, field_ref, t, field_sem).start()
        moving(cotangent_hbm, cotangent_ref, t, cotangent_sem).start()
    second_inverse(parts_ref, inverse_ref[...], planes_ref)
    scale = 0.7978845608028654
    cubic = scale * 0.044715

    def step(t, carry):
        moving(field_hbm, field_ref, t, field_sem).wait()
        moving(cotangent_hbm, cotangent_ref, t, cotangent_sem).wait()
        y = pl.ds(pl.multiple_of((t % 2) * 16, 16), 16)
        rows = pl.ds(pl.multiple_of(t * 16, 16), 16)
        planes = planes_ref[:, rows, :].reshape(C * 16, 128)
        left = jnp.concatenate([planes, wide_ref[...]], axis=1)
        slopes = []
        for x in range(2):
            field = field_ref[:, x, t // 2, y, :].reshape(C * 16, N)
            right = jnp.concatenate([synth_ref[:, x * N : (x + 1) * N], field], axis=0)
            values = dot(left, right)
            pieces = []
            for c in range(C):
                value = values[c * 16 : (c + 1) * 16] + bias_ref[c]
                square = value * value
                half = 0.5 + 0.5 * jnp.tanh(value * (scale + cubic * square))
                activated = value * half
                activated_ref[c, x, t // 2, y, :] = activated.astype(BF)
                d_inner = (2.0 * scale) + (6.0 * cubic) * square
                d_gelu = half + (activated * (1.0 - half)) * d_inner
                pieces.append((cotangent_ref[c, x, t // 2, y, :].astype(F32) * d_gelu).astype(BF))
            slope = jnp.concatenate(pieces, axis=0)
            slopes.append(slope)
            mixed = dot(wide_back_ref[...], slope).astype(BF)
            mixed_ref[:, x, t // 2, y, :] = mixed.reshape(C, 16, N)
        moving(activated_ref, activated_hbm, t, activated_sem).start()
        response = dot(jnp.concatenate(slopes, axis=1), depth_ref[...])
        turned_ref[:, rows, :] = response.astype(BF).reshape(C, 16, 256)
        return carry

    lax.fori_loop(0, 8, step, 0)
    second_forward(turned_ref, table_ref[...], out_ref, 0, C)
    for t in range(8):
        moving(activated_ref, activated_hbm, t, activated_sem).wait()


def local(parts, field, cotangent, *operands):
    return pl.pallas_call(
        local_kernel,
        in_specs=[VMEM, HBM, HBM] + [VMEM] * 6 + [pl.BlockSpec(memory_space=pltpu.SMEM)],
        out_specs=[HBM, VMEM, VMEM],
        out_shape=[
            pltpu.HBM(GRID, BF),
            jax.ShapeDtypeStruct(GRID, BF),
            jax.ShapeDtypeStruct((8, PARTS, 128), BF),
        ],
        scratch_shapes=[pltpu.VMEM((C, 128, 128), BF), pltpu.VMEM((C, 128, 256), BF)]
        + [pltpu.VMEM(GRID, BF)] * 3
        + [pltpu.SemaphoreType.DMA((8,))] * 3,
        compiler_params=params(24),
        cost_estimate=cost(3 * 10**9, 12 * MIB, 1310720),
        name="local",
    )(parts, *in_hbm(field, cotangent), *operands)


def local_back_kernel(
    parts_ref,
    mixed_ref,
    synth_ref,
    inverse_ref,
    perm_ref,
    out_hbm,
    grad_hbm,
    planes_ref,
    modes_ref,
    out_ref,
    grad_ref,
    out_sem,
    grad_sem,
):
    pair = parts_ref[:, PARTS:, :].reshape(128, 128)
    for i in range(4):
        modes_ref[pl.ds(i, 128, stride=4), :] = dot_tn(pair, perm_ref[i].astype(BF))
    r0 = modes_ref[8 * M : 8 * M + 4 * C, :]
    r1 = modes_ref[12 * M : 12 * M + 4 * C, :]

    def outer(t):
        return pltpu.make_async_copy(
            grad_ref.at[:, pl.ds(t * 5, 5)], grad_hbm.at[:, pl.ds(t * 5, 5)], grad_sem.at[t]
        )

    for c in range(C):
        s0 = jnp.concatenate([modes_ref[c * 4 : c * 4 + 4, :]] * C, axis=0)
        s1 = jnp.concatenate([modes_ref[4 * M + c * 4 : 4 * M + c * 4 + 4, :]] * C, axis=0)
        grad_ref[0, c] = s0 * r0 + s1 * r1
        grad_ref[1, c] = s0 * r1 - s1 * r0
        if c % 5 == 4:
            outer(c // 5).start()

    second_inverse(parts_ref, inverse_ref[...], planes_ref)

    def step(t, carry):
        y = pl.ds(pl.multiple_of((t % 2) * 16, 16), 16)
        rows = pl.ds(pl.multiple_of(t * 16, 16), 16)
        planes = planes_ref[:, rows, :].reshape(C * 16, 128)
        spatial = dot(planes, synth_ref[...])
        for x in range(2):
            for c in range(C):
                value = spatial[c * 16 : (c + 1) * 16, x * N : (x + 1) * N]
                value = value + mixed_ref[c, x, t // 2, y, :].astype(F32)
                out_ref[c, x, t // 2, y, :] = value.astype(BF)
        moving(out_ref, out_hbm, t, out_sem).start()
        return carry

    lax.fori_loop(0, 8, step, 0, unroll=4)
    for t in range(8):
        moving(out_ref, out_hbm, t, out_sem).wait()
    for t in range(4):
        outer(t).wait()


def local_back(parts, mixed, *tables):
    grad = (2, C, 4 * C, M)
    return pl.pallas_call(
        local_back_kernel,
        in_specs=[VMEM] * (2 + len(tables)),
        out_specs=[HBM, HBM],
        out_shape=[pltpu.HBM(GRID, BF), pltpu.HBM(grad, F32)],
        scratch_shapes=[
            pltpu.VMEM((C, 128, 128), BF),
            pltpu.VMEM((512, M), F32),
            pltpu.VMEM(GRID, BF),
            pltpu.VMEM(grad, F32),
            pltpu.SemaphoreType.DMA((8,)),
            pltpu.SemaphoreType.DMA((4,)),
        ],
        compiler_params=params(24),
        cost_estimate=cost(2 * 10**9, 6 * MIB),
        name="local_back",
    )(parts, mixed, *tables)


def exchange(value, axis):
    return lax.all_to_all(value, axis, split_axis=0, concat_axis=0, tiled=True)


def shards(field, cotangent, spectral_weight, local_weight, local_bias):
    forward, inverse = depth_tables()
    forward_b, inverse_b = analysis_depth(forward), analysis_depth(inverse.T)
    synth_f, synth_b = bf16(inverse), bf16(forward.T)
    second, second_back = second_tables()
    first = first_table()
    block = lax.axis_index("narrow").astype(jnp.int32).reshape(1)

    sizes = {"J": 8, "j": 4, "i": 4}
    perm_line = line_table()
    perm_weight = permutation("Jji", "iJj", sizes)
    perm_modes = permutation("Jji", "jJi", sizes)
    perm_grad = np.stack([perm_weight[:, i * M : (i + 1) * M] for i in range(4)])

    shape = field.shape
    grid_field = field.reshape(GRID)
    grid_cotangent = cotangent.reshape(GRID)

    weight = jnp.transpose(spectral_weight, (0, 1, 2, 3, 5, 4)).reshape(8 * C * C, M)
    parts = exchange(analyse(block, grid_field, weight, forward_b, second, perm_grad), "narrow")
    weight, synth, depth, table, table_back, back, wide, wide_back = weight_in(
        block, parts, perm_modes, synth_f, inverse_b, second, second_back, synth_b, local_weight
    )
    lines = exchange(gather(parts, perm_line, CARRY_ROWS), "wide")
    lines, spectrum = mix(lines, weight, first)
    lines = exchange(lines, "wide")
    parts = exchange(scatter(lines, perm_line), "narrow")
    activated, mixed, parts = local(
        parts,
        grid_field,
        grid_cotangent,
        synth,
        depth,
        table,
        table_back,
        wide,
        wide_back,
        local_bias,
    )
    parts = exchange(parts, "narrow")
    lines = exchange(gather(parts, perm_line, FIELD_ROWS), "wide")
    lines, pair = mix_back(lines, weight, first, spectrum, perm_modes)
    lines = exchange(lines, "wide")
    parts = exchange(scatter(lines, perm_line, pair), "narrow")
    field_grad, weight_grad = local_back(parts, mixed, back, table_back, perm_grad)
    return (
        activated.reshape(shape),
        field_grad.reshape(shape),
        weight_grad.reshape(spectral_weight.shape),
    )


def solution(mesh):
    return jax.shard_map(
        shards,
        mesh=mesh,
        in_specs=(
            P(None, "wide", "narrow", None),
            P(None, "wide", "narrow", None),
            P(None, None, None, "narrow", None, "wide"),
            P(),
            P(),
        ),
        out_specs=(
            P(None, "wide", "narrow", None),
            P(None, "wide", "narrow", None),
            P(None, None, None, "narrow", None, "wide"),
        ),
        check_vma=False,
    )
```
